256 devices in a mesh: net: 4 (over x_lo, core), ctg: 64 (over z, x_hi, y).
Axes of the slice: x: 4 (x_hi: 2, x_lo: 2; x = x_hi * 2 + x_lo), y: 4, z: 8, core: 2. Of those that a mesh axis runs over, the one named last changes fastest.
Arguments:
- angle_dir: float32 [256, 16, 16384], P('ctg', None, 'net'), may hold values from -6 to 6
- dispatch_dir: float32 [16, 5120], P(None, 'net'), may hold values from -6 to 6
- barrier: bfloat16 [256, 16, 16384], P('ctg', None, 'net'), may hold values from 0.19921875 to 2
- angle_reg: float32 [16, 16384], P(None, 'net'), may hold values from 0.5 to 2
- dispatch_reg: float32 [16, 5120], P(None, 'net'), may hold values from 1 to 10
- susceptance: float32 [22528], P('net'), may hold values from 0.2 to 2
- from_bus: int32 [22528], P('net'), may hold values from 0 to 16383, as said below
- to_bus: int32 [22528], P('net'), may hold values from 1 to 16383, as said below
- outage: int32 [256], P('ctg'), may hold values from 0 to 22527
- gen_bus: int32 [5120], P('net'), may hold values from 0 to 16383, as said below
Outputs:
- angle_out: float32 [256, 16, 16384], P('ctg', None, 'net')
- dispatch_out: float32 [16, 5120], P(None, 'net')
The draws below stay inside these ranges and needn't reach their ends.
Inputs may be any that keep to these rules, and one draw needn't show every extreme that they name: Branch k lies in network block k // 5632: from_bus[k] is a bus of that block, numbered k's block times 4096 onward. to_bus[k] - from_bus[k] is between 1 and 128, and equals 128 for some branch of every block. `gen_bus`: generator g sits at a bus of network block g // 1280.
All inputs are finite; a program needn't handle non-finite values.
Results may differ from the reference program's by a relative error of at most 0.0003.
Values sent between devices are 32-bit elements; how exact they have to be, the bound alone decides.
No kernel may reach another device: no remote copies, remote signals or barrier semaphores. Data moves between devices by JAX's collectives and lax.ppermute only.
A program may use at most 64 MiB of HBM per device.

```python
import math
import jax
import jax.numpy as jnp
from jax import lax

BUS_DEV = 4096
BR_DEV = 5632
G_DEV = 1280
RIM = 128
PERIODS = 16
BUS = 16384
BR = 22528
GENS = 5120
CTG = 256


def branch_ends(key):
    block = jnp.arange(BR, dtype=jnp.int32) // BR_DEV
    local = jnp.arange(BR, dtype=jnp.int32) % BR_DEV
    start = jax.random.randint(jax.random.fold_in(key, 11), (BR,), 0, BUS_DEV).astype(jnp.int32)
    offset = jax.random.randint(jax.random.fold_in(key, 12), (BR,), 1, RIM + 1).astype(jnp.int32)
    start = jnp.where(local == BR_DEV - 1, BUS_DEV - 1, start)
    offset = jnp.where(local == BR_DEV - 1, RIM, offset)
    first = jnp.minimum(block * BUS_DEV + start, BUS - 1 - RIM)
    return (first, first + offset)


def draw_from_bus(key, part):
    return branch_ends(key)[0]


def draw_to_bus(key, part):
    return branch_ends(key)[1]


def draw_gen_bus(key, part):
    block = jnp.arange(GENS, dtype=jnp.int32) // G_DEV
    place = jax.random.randint(jax.random.fold_in(key, 21), (GENS,), 0, BUS_DEV).astype(jnp.int32)
    return block * BUS_DEV + place


def place_ends(values, key, low, high):
    shape = values.shape
    spot = [jax.random.randint(jax.random.fold_in(key, axis), (), 0, shape[axis]) for axis in range(len(shape))]
    values = values.at[tuple(spot)].set(low)
    longest = shape.index(max(shape))
    spot[longest] = (spot[longest] + 1) % shape[longest]
    return values.at[tuple(spot)].set(high)


def steps_of(own_key, dims, pieces, low, high):
    loudness, own = 1.0, jax.random.fold_in(own_key, 6)
    for axis_at, parts in pieces:
        draws = jnp.exp(jax.random.uniform(jax.random.fold_in(own, axis_at), (parts,), jnp.float32, low / len(pieces), high / len(pieces)))
        loudness = loudness * jnp.repeat(draws, dims[axis_at] // parts).reshape([-1 if axis == axis_at else 1 for axis in range(len(dims))])
    return loudness


def noise(rng, dims, deviation, most, pieces=(), kind=jnp.bfloat16):
    values = jax.random.normal(rng, dims, jnp.float32) * deviation
    if len(pieces) > 0:
        values = steps_of(rng, dims, pieces, -0.22, 0.18) * values
    return jnp.clip(values, min=-most, max=most).astype(kind)


def setup_inputs(seed: int = 0) -> dict:
    arg_keys = jax.random.split(jax.random.key(seed), 11)
    angle_dir = noise(arg_keys[0], (CTG, PERIODS, BUS), 1.0, 6.0, ((0, 64), (2, 4)), jnp.float32)
    dispatch_dir = noise(arg_keys[1], (PERIODS, GENS), 1.0, 6.0, ((1, 4),), jnp.float32)
    barrier = jnp.clip(jnp.exp(math.log(2.0) - 2.306499 * jax.random.uniform(arg_keys[2], (CTG, PERIODS, BUS), jnp.float32) ** steps_of(arg_keys[2], (CTG, PERIODS, BUS), ((0, 64), (2, 4)), -0.2, 0.2)), 0.19921875, 2.0).astype(jnp.bfloat16)
    angle_reg = jnp.clip(jnp.exp(math.log(2.0) - 1.3862944 * jax.random.uniform(arg_keys[3], (PERIODS, BUS), jnp.float32) ** steps_of(arg_keys[3], (PERIODS, BUS), ((1, 4),), -0.2, 0.2)), 0.5, 2.0)
    dispatch_reg = jnp.clip(jnp.exp(math.log(10.0) - 2.3025851 * jax.random.uniform(arg_keys[4], (PERIODS, GENS), jnp.float32) ** steps_of(arg_keys[4], (PERIODS, GENS), ((1, 4),), -0.2, 0.2)), 1.0, 10.0)
    susceptance = jnp.clip(jnp.exp(math.log(2.0) - 2.3025851 * jax.random.uniform(arg_keys[5], (BR,), jnp.float32) ** steps_of(arg_keys[5], (BR,), ((0, 4),), -0.2, 0.2)), 0.2, 2.0)
    from_bus = draw_from_bus(jax.random.fold_in(arg_keys[10], 71), 0)
    to_bus = draw_to_bus(jax.random.fold_in(arg_keys[10], 71), 0)
    outage = place_ends(jax.random.randint(arg_keys[8], (CTG,), 0, BR), jax.random.fold_in(arg_keys[8], 1), 0, BR - 1).astype(jnp.int32)
    gen_bus = draw_gen_bus(jax.random.fold_in(arg_keys[10], 71), 0)
    return {"angle_dir": angle_dir, "dispatch_dir": dispatch_dir, "barrier": barrier, "angle_reg": angle_reg, "dispatch_reg": dispatch_reg, "susceptance": susceptance, "from_bus": from_bus, "to_bus": to_bus, "outage": outage, "gen_bus": gen_bus}


def apply_network(field, susc, from_bus, to_bus):
    branch_flow = susc[None, :] * (field[:, from_bus] - field[:, to_bus])
    result = jnp.zeros(field.shape, jnp.float32)
    result = result.at[:, from_bus].add(branch_flow)
    return result.at[:, to_bus].add(-branch_flow)


def reference(angle_dir, dispatch_dir, barrier, angle_reg, dispatch_reg, susceptance, from_bus, to_bus, outage, gen_bus):
    inject = jnp.zeros((PERIODS, BUS), jnp.float32).at[:, gen_bus].add(dispatch_dir)
    branch_ids = jnp.arange(BR, dtype=jnp.int32)

    def one_case(carry, items):
        angle_case, barrier_case, outage_case = items
        susc = jnp.where(branch_ids == outage_case, 0.0, susceptance).astype(jnp.float32)
        resid = apply_network(angle_case, susc, from_bus, to_bus) - inject
        weighted = barrier_case.astype(jnp.float32) * resid
        result = apply_network(weighted, susc, from_bus, to_bus) + angle_reg * angle_case
        return carry + weighted, result

    total, angle_out = lax.scan(one_case, jnp.zeros((PERIODS, BUS), jnp.float32), (angle_dir, barrier, outage))
    total = total / float(CTG)
    dispatch_out = dispatch_reg * dispatch_dir - total[:, gen_bus]
    return angle_out, dispatch_out
```

```python
import jax
import jax.numpy as jnp
from jax import lax
from jax.experimental import pallas as pl
from jax.experimental.pallas import tpu as pltpu
from jax.sharding import PartitionSpec as P

BUS_DEV = 4096
BR_DEV = 5632
G_DEV = 1280
RIM = 128
PERIODS = 16
TILES = BUS_DEV // RIM
BR_ROWS = BR_DEV // RIM
CASES = 4
ROWS = CASES * PERIODS
VMEM_LIMIT = 56 * 1024 * 1024
BF16 = jnp.bfloat16
F32 = jnp.float32


def split(value):
    high = value.astype(BF16)
    low = (value - high.astype(F32)).astype(BF16)
    return high, low


def dot_last(left, right):
    return lax.dot_general(
        left, right, (((1,), (1,)), ((), ())), preferred_element_type=F32
    )


def dot_plain(left, right):
    return jnp.dot(left, right, preferred_element_type=F32)


def whole(ref_space=pltpu.VMEM):
    return pl.BlockSpec(memory_space=ref_space)


def pack_kernel(from_ref, to_ref, susc_ref, last_ref, out_ref):
    for row in range(BR_ROWS):
        cols = pl.ds(row * RIM, RIM)
        out_ref[row : row + 1, :] = from_ref[:, cols].astype(F32)
        out_ref[BR_ROWS + row : BR_ROWS + row + 1, :] = to_ref[:, cols].astype(F32)
        out_ref[2 * BR_ROWS + row : 2 * BR_ROWS + row + 1, :] = susc_ref[:, cols]
    out_ref[136:200, :] = last_ref[...]


def pack(from_bus, to_bus, susceptance, field):
    row = pl.BlockSpec((1, BR_DEV), lambda i: (0, 0))
    return pl.pallas_call(
        pack_kernel,
        grid=(1,),
        in_specs=[row, row, row, pl.BlockSpec((ROWS, RIM), lambda i: (0, TILES - 1))],
        out_specs=pl.BlockSpec((200, RIM), lambda i: (0, 0)),
        out_shape=jax.ShapeDtypeStruct((200, RIM), F32),
        name="pack",
    )(from_bus, to_bus, susceptance, field)


def end_rows(to_pos, susc):
    high, low = split(susc)
    spots = lax.broadcasted_iota(jnp.int32, (RIM, to_pos.shape[1]), 0)
    hit = spots == to_pos
    zero = jnp.zeros((), BF16)
    return jnp.concatenate(
        [jnp.where(hit, high, zero), jnp.where(hit, low, zero)], axis=0
    )


def wide_tiles(block):
    rows = lax.broadcasted_iota(jnp.int32, (RIM, RIM), 0)
    cols = lax.broadcasted_iota(jnp.int32, (RIM, RIM), 1)
    inside = cols > rows
    return jnp.concatenate(
        [jnp.where(inside, block, 0.0), jnp.where(inside, 0.0, block)], axis=1
    )


BUILD_ROWS = 512


def band_kernel(from_ref, to_ref, susc_ref, base_ref, high_ref, low_ref, ends_ref):
    step = pl.program_id(0)

    @pl.when(step == 0)
    def _():
        ends_ref[...] = end_rows((to_ref[...] - base_ref[0]) % RIM, susc_ref[...])

    from_local = from_ref[...] - base_ref[0] - step * BUILD_ROWS
    spots = lax.broadcasted_iota(jnp.int32, (BUILD_ROWS, BR_DEV), 0)
    starts = jnp.where(spots == from_local, 1.0, 0.0).astype(BF16)
    both = dot_last(starts, ends_ref[...])
    block = both[:, :RIM] + both[:, RIM:]
    for tile in range(BUILD_ROWS // RIM):
        high, low = split(wide_tiles(block[tile * RIM : (tile + 1) * RIM]))
        high_ref[tile] = high
        low_ref[tile] = low


def build_band(from_bus, to_bus, susceptance, base):
    row = pl.BlockSpec((1, BR_DEV), lambda i: (0, 0))
    step = BUILD_ROWS // RIM
    out = pl.BlockSpec((step, RIM, 2 * RIM), lambda i: (i, 0, 0))
    shape = jax.ShapeDtypeStruct((TILES, RIM, 2 * RIM), BF16)
    return pl.pallas_call(
        band_kernel,
        grid=(TILES // step,),
        in_specs=[row, row, row, whole(pltpu.SMEM)],
        out_specs=[out, out],
        out_shape=[shape, shape],
        scratch_shapes=[pltpu.VMEM((2 * RIM, BR_DEV), BF16)],
        compiler_params=pltpu.CompilerParams(vmem_limit_bytes=VMEM_LIMIT),
        cost_estimate=pl.CostEstimate(
            flops=2 * BUS_DEV * BR_DEV * 2 * RIM, bytes_accessed=4 << 20, transcendentals=0
        ),
        name="band",
    )(from_bus, to_bus, susceptance, base)


def outage_row(from_at, to_at, tile):
    spots = lax.broadcasted_iota(jnp.int32, (1, RIM), 1) + (tile + 1) * RIM
    return jnp.where(spots == from_at, 1.0, 0.0) - jnp.where(spots == to_at, 1.0, 0.0)


def stack_parts(values):
    high, low = split(values)
    return jnp.concatenate([high, low, jnp.ones((16, RIM), BF16)], axis=0)


def apply_tiles(tile_of, stacks, high_ref, low_ref, cross_high, cross_low, ends, susc, emit):
    flows = [jnp.zeros((PERIODS, RIM), F32) for _ in range(CASES)]
    for tile in range(-1, TILES + 1):
        value = tile_of(tile)
        stacks[tile + 1] = stack_parts(value)
        for case in range(CASES):
            mask = outage_row(ends[case][0], ends[case][1], tile)
            flows[case] += value[case * PERIODS : (case + 1) * PERIODS] * mask
    drops = [
        susc[case] * jnp.sum(flows[case], axis=1, keepdims=True) for case in range(CASES)
    ]
    before = dot_plain(stacks[0], cross_high) + dot_plain(stacks[0], cross_low)
    for tile in range(TILES):
        own = stacks[tile + 1]
        high, low = high_ref[tile], low_ref[tile]
        ahead = dot_plain(own, high) + dot_plain(own, low)
        near = jnp.concatenate([own, stacks[tile + 2]], axis=1)
        sums = before + ahead[:, :RIM] + dot_last(near, high) + dot_last(near, low)
        before = ahead[:, RIM:]
        degrees = sums[2 * ROWS : 2 * ROWS + 1]
        value = tile_of(tile)
        result = degrees * value - (sums[:ROWS] + sums[ROWS : 2 * ROWS])
        parts = []
        for case in range(CASES):
            mask = outage_row(ends[case][0], ends[case][1], tile)
            parts.append(
                result[case * PERIODS : (case + 1) * PERIODS] - drops[case] * mask
            )
        emit(tile, jnp.concatenate(parts, axis=0))


def resid_kernel(
    place_ref,
    outage_ref,
    field_ref,
    barrier_ref,
    high_ref,
    low_ref,
    from_ref,
    to_ref,
    susc_ref,
    left_ref,
    right_ref,
    dispatch_ref,
    gen_ref,
    weighted_ref,
    first_ref,
    last_ref,
    partial_ref,
    cross_high_ref,
    cross_low_ref,
    ends_ref,
    stacks,
    inject,
    total,
):
    block = place_ref[0]
    base = block * BUS_DEV
    keep = jnp.where(block > 0, 1.0, 0.0)
    left_from = jnp.concatenate(
        [left_ref[r : r + 1] for r in range(BR_ROWS)], axis=1
    ).astype(jnp.int32)
    left_to = jnp.concatenate(
        [left_ref[BR_ROWS + r : BR_ROWS + r + 1] for r in range(BR_ROWS)], axis=1
    ).astype(jnp.int32)
    left_susc = jnp.concatenate(
        [left_ref[2 * BR_ROWS + r : 2 * BR_ROWS + r + 1] for r in range(BR_ROWS)], axis=1
    )
    crosses = left_to >= base
    left_ends = end_rows(
        (left_to - base) % RIM, jnp.where(crosses, left_susc, 0.0) * keep
    )
    spots = lax.broadcasted_iota(jnp.int32, (RIM, BR_DEV), 0) + (base - RIM)
    starts = jnp.where(spots == left_from, 1.0, 0.0).astype(BF16)
    both = dot_last(starts, left_ends)
    cross_high, cross_low = split(both[:, :RIM] + both[:, RIM:])
    cross_high_ref[...] = cross_high
    cross_low_ref[...] = cross_low

    branch = lax.broadcasted_iota(jnp.int32, (1, BR_DEV), 1)
    ends, susc = [], []
    for case in range(CASES):
        own_hit = branch == outage_ref[case] - block * BR_DEV
        left_hit = branch == outage_ref[case] - (block - 1) * BR_DEV
        pick = lambda own, left: (
            jnp.sum(jnp.where(own_hit, own, 0.0), axis=1, keepdims=True)
            + jnp.sum(jnp.where(left_hit, left, 0.0), axis=1, keepdims=True) * keep
        )
        start = pick(from_ref[...].astype(F32), left_from.astype(F32)).astype(jnp.int32)
        end = pick(to_ref[...].astype(F32), left_to.astype(F32)).astype(jnp.int32)
        ends.append((start - base + RIM, end - base + RIM))
        susc.append(pick(susc_ref[...], left_susc))
        ends_ref[case : case + 1, :] = jnp.broadcast_to(ends[case][0].astype(F32), (1, RIM))
        ends_ref[4 + case : 5 + case, :] = jnp.broadcast_to(
            ends[case][1].astype(F32), (1, RIM)
        )
        ends_ref[8 + case : 9 + case, :] = jnp.broadcast_to(susc[case], (1, RIM))

    gen = gen_ref[...] - base
    gen_tile = gen // RIM
    spots = lax.broadcasted_iota(jnp.int32, (RIM, G_DEV), 0)
    gen_spots = jnp.where(spots == gen % RIM, 1.0, 0.0).astype(BF16)
    dispatch = dispatch_ref[...]
    dispatch_high, dispatch_low = split(dispatch)
    zero = jnp.zeros((), BF16)
    for part in range(4):
        tiles = range(part * TILES // 4, (part + 1) * TILES // 4)
        picked = jnp.concatenate(
            [jnp.where(gen_tile == tile, dispatch_high, zero) for tile in tiles]
            + [jnp.where(gen_tile == tile, dispatch_low, zero) for tile in tiles],
            axis=0,
        )
        spread = dot_last(picked, gen_spots)
        half = spread.shape[0] // 2
        inject[part * half : (part + 1) * half] = spread[:half] + spread[half:]

    def tile_of(tile):
        if tile < 0:
            return left_ref[136:200]
        if tile == TILES:
            return right_ref[...]
        return field_ref[:, tile * RIM : (tile + 1) * RIM]

    def emit(tile, result):
        rows = slice(tile * PERIODS, (tile + 1) * PERIODS)
        taken = inject[rows]
        resid = result - jnp.concatenate([taken] * CASES, axis=0)
        weighted = barrier_ref[:, tile * RIM : (tile + 1) * RIM].astype(F32) * resid
        weighted_ref[:, tile * RIM : (tile + 1) * RIM] = weighted
        if tile == 0:
            first_ref[...] = weighted
        if tile == TILES - 1:
            last_ref[...] = weighted
        total[rows] = (
            weighted[0:16] + weighted[16:32] + (weighted[32:48] + weighted[48:64])
        )

    apply_tiles(
        tile_of, stacks, high_ref, low_ref, cross_high, cross_low, ends, susc, emit
    )

    at_gens = jnp.zeros((PERIODS, G_DEV), F32)
    for part in range(4):
        size = TILES * PERIODS // 4
        high, low = split(total[part * size : (part + 1) * size])
        both = dot_plain(jnp.concatenate([high, low], axis=0), gen_spots)
        for k in range(TILES // 4):
            tile = part * TILES // 4 + k
            rows = slice(k * PERIODS, (k + 1) * PERIODS)
            value = both[rows] + both[size + k * PERIODS : size + (k + 1) * PERIODS]
            at_gens += jnp.where(gen_tile == tile, value, 0.0)
    partial_ref[...] = at_gens


def residuals(place, outage, field, barrier, band, raw, halos, dispatch, gen_bus):
    tile = jax.ShapeDtypeStruct((ROWS, RIM), F32)
    return pl.pallas_call(
        resid_kernel,
        in_specs=[whole(pltpu.SMEM)] * 2 + [whole()] * 11,
        out_specs=[whole()] * 7,
        out_shape=[
            jax.ShapeDtypeStruct((ROWS, BUS_DEV), F32),
            tile,
            tile,
            jax.ShapeDtypeStruct((PERIODS, G_DEV), F32),
            jax.ShapeDtypeStruct((RIM, RIM), BF16),
            jax.ShapeDtypeStruct((RIM, RIM), BF16),
            jax.ShapeDtypeStruct((16, RIM), F32),
        ],
        scratch_shapes=[
            pltpu.VMEM((TILES + 2, 2 * ROWS + 16, RIM), BF16),
            pltpu.VMEM((TILES * PERIODS, RIM), F32),
            pltpu.VMEM((TILES * PERIODS, RIM), F32),
        ],
        compiler_params=pltpu.CompilerParams(vmem_limit_bytes=VMEM_LIMIT),
        cost_estimate=pl.CostEstimate(flops=4 << 30, bytes_accessed=8 << 20, transcendentals=0),
        name="resid",
    )(place, outage, field, barrier, *band, *raw, *halos, dispatch, gen_bus)


def angle_kernel(
    weighted_ref,
    field_ref,
    reg_ref,
    high_ref,
    low_ref,
    cross_high_ref,
    cross_low_ref,
    ends_ref,
    left_ref,
    right_ref,
    out_ref,
    stacks,
):
    ends, susc = [], []
    for case in range(CASES):
        start = ends_ref[case : case + 1, 0:1].astype(jnp.int32)
        end = ends_ref[4 + case : 5 + case, 0:1].astype(jnp.int32)
        ends.append((start, end))
        susc.append(ends_ref[8 + case : 9 + case, 0:1])

    def tile_of(tile):
        if tile < 0:
            return left_ref[...]
        if tile == TILES:
            return right_ref[...]
        return weighted_ref[:, tile * RIM : (tile + 1) * RIM]

    def emit(tile, result):
        cols = slice(tile * RIM, (tile + 1) * RIM)
        scale = jnp.concatenate([reg_ref[:, cols]] * CASES, axis=0)
        out_ref[:, cols] = result + scale * field_ref[:, cols]

    apply_tiles(
        tile_of,
        stacks,
        high_ref,
        low_ref,
        cross_high_ref[...],
        cross_low_ref[...],
        ends,
        susc,
        emit,
    )


def angles(weighted, field, reg, band, cross, ends, halos):
    return pl.pallas_call(
        angle_kernel,
        in_specs=[whole()] * 10,
        out_specs=whole(),
        out_shape=jax.ShapeDtypeStruct((ROWS, BUS_DEV), F32),
        scratch_shapes=[pltpu.VMEM((TILES + 2, 2 * ROWS + 16, RIM), BF16)],
        compiler_params=pltpu.CompilerParams(vmem_limit_bytes=VMEM_LIMIT),
        cost_estimate=pl.CostEstimate(flops=4 << 30, bytes_accessed=8 << 20, transcendentals=0),
        name="angles",
    )(weighted, field, reg, *band, *cross, ends, *halos)


def shifted(block, distance):
    size = lax.axis_size("net")
    return lax.ppermute(block, "net", [(i, (i + distance) % size) for i in range(size)])


def sum_cases(value):
    size = lax.axis_size("ctg")
    for mask in (1, 3, 4, 8, 16, 56):
        value = value + lax.ppermute(value, "ctg", [(i, i ^ mask) for i in range(size)])
    return value


def body(
    angle_dir,
    dispatch_dir,
    barrier,
    angle_reg,
    dispatch_reg,
    susceptance,
    from_bus,
    to_bus,
    outage,
    gen_bus,
):
    block = lax.axis_index("net")
    place = jnp.reshape(block, (1,)).astype(jnp.int32)
    field = angle_dir.reshape(ROWS, BUS_DEV)
    weights = barrier.reshape(ROWS, BUS_DEV)
    raw = (
        from_bus.reshape(1, BR_DEV),
        to_bus.reshape(1, BR_DEV),
        susceptance.reshape(1, BR_DEV),
    )
    packed = pack(*raw, field)
    left = shifted(packed, 1)
    right = shifted(field[:, :RIM], -1)
    band = build_band(*raw, place * BUS_DEV)
    weighted, first, last, partial, cross_high, cross_low, ends = residuals(
        place,
        outage,
        field,
        weights,
        band,
        raw,
        (left, right),
        dispatch_dir,
        gen_bus.reshape(1, G_DEV),
    )
    halos = (shifted(last, 1), shifted(first, -1))
    summed = sum_cases(partial)
    angle_out = angles(
        weighted, field, angle_reg, band, (cross_high, cross_low), ends, halos
    )
    case_count = float(CASES * lax.axis_size("ctg"))
    dispatch_out = dispatch_reg * dispatch_dir - summed / case_count
    return (angle_out.reshape(angle_dir.shape), dispatch_out)


def solution(mesh):
    placed = (
        P("ctg", None, "net"),
        P(None, "net"),
        P("ctg", None, "net"),
        P(None, "net"),
        P(None, "net"),
        P("net"),
        P("net"),
        P("net"),
        P("ctg"),
        P("net"),
    )
    return jax.shard_map(
        body,
        mesh=mesh,
        in_specs=placed,
        out_specs=(P("ctg", None, "net"), P(None, "net")),
        check_vma=False,
    )
```

```python
import jax
import jax.numpy as jnp
from jax import lax
from jax.experimental import pallas as pl
from jax.experimental.pallas import tpu as pltpu
from jax.sharding import PartitionSpec as P

BUS_DEV = 4096
BR_DEV = 5632
G_DEV = 1280
RIM = 128
PERIODS = 16
TILES = BUS_DEV // RIM
BR_ROWS = BR_DEV // RIM
PAIRS = TILES // 2
CASES = 4
ROWS = CASES * PERIODS
VMEM_LIMIT = 20 * 1024 * 1024
SLOTS = 256
GROUPS = 64
WORK = 256
BF16 = jnp.bfloat16
F32 = jnp.float32


def split(value):
    high = value.astype(BF16)
    low = (value - high.astype(F32)).astype(BF16)
    return high, low


def dot_last(left, right):
    return lax.dot_general(
        left, right, (((1,), (1,)), ((), ())), preferred_element_type=F32
    )


def dot_plain(left, right):
    return jnp.dot(left, right, preferred_element_type=F32)


def whole(ref_space=pltpu.VMEM):
    return pl.BlockSpec(memory_space=ref_space)


def one_hot(rows, index):
    spots = lax.broadcasted_iota(jnp.int32, (rows, index.shape[1]), 0)
    return spots == index


def ones_at(mask):
    return jnp.where(mask, 1.0, 0.0).astype(BF16)


def held_at(mask, values):
    return jnp.where(mask, values, 0.0).astype(BF16)


def parts_of(values):
    high = values.astype(BF16).astype(F32)
    return high, values - high


def as_row(ref):
    return ref[...].reshape(1, ref.shape[0])


def pack_kernel(from_ref, to_ref, susc_ref, last_ref, lead_ref, out_ref, first_ref):
    for part, ref in enumerate((from_ref, to_ref, susc_ref)):
        row = as_row(ref).astype(F32)
        for k in range(BR_ROWS):
            at = part * BR_ROWS + k
            out_ref[at : at + 1, :] = row[:, k * RIM : (k + 1) * RIM]
    out_ref[136:200, :] = last_ref[...]
    first_ref[...] = lead_ref[...]


def pack(from_bus, to_bus, susceptance, field):
    row = pl.BlockSpec((BR_DEV,), lambda i: (0,))
    return pl.pallas_call(
        pack_kernel,
        grid=(1,),
        in_specs=[
            row,
            row,
            row,
            pl.BlockSpec((ROWS, RIM), lambda i: (0, TILES - 1)),
            pl.BlockSpec((ROWS, RIM), lambda i: (0, 0)),
        ],
        out_specs=[whole(), whole()],
        out_shape=[pltpu.VMEM((200, RIM), F32), pltpu.VMEM((ROWS, RIM), F32)],
        compiler_params=pltpu.CompilerParams(vmem_limit_bytes=4 << 20),
        name="pack",
    )(from_bus, to_bus, susceptance, field, field)


def tile_of_group(starts_row, to_row, high_row, low_row):
    starts = ones_at(one_hot(RIM, starts_row))
    hit = one_hot(RIM, to_row)
    ends = jnp.concatenate([held_at(hit, high_row), held_at(hit, low_row)], axis=0)
    both = dot_last(starts, ends)
    return both[:, :RIM] + both[:, RIM:]


def band_kernel(
    base_ref, from_ref, to_ref, susc_ref, high_ref, low_ref, degree_ref, tiles, table
):
    base = base_ref[0] * BUS_DEV
    from_local = as_row(from_ref) - base
    tile = from_local // RIM
    tile_hit = one_hot(TILES, tile)
    member = jnp.where(tile_hit, 1.0, 0.0)
    packed = member.astype(BF16)
    chunks = BR_DEV // WORK
    rows = lax.broadcasted_iota(jnp.int32, (WORK, WORK), 0)
    cols = lax.broadcasted_iota(jnp.int32, (WORK, WORK), 1)
    upto = jnp.where(rows <= cols, 1.0, 0.0).astype(BF16)
    counts = dot_plain(
        jnp.concatenate([packed[:, c * WORK : (c + 1) * WORK] for c in range(chunks)], axis=0),
        upto,
    )
    seen = jnp.zeros((TILES, 1), F32)
    ranks = []
    for c in range(chunks):
        local = counts[c * TILES : (c + 1) * TILES]
        part = member[:, c * WORK : (c + 1) * WORK] * (local + seen)
        ranks.append(jnp.sum(part, axis=0, keepdims=True) - 1.0)
        seen = seen + local[:, WORK - 1 : WORK]
    rank = jnp.concatenate(ranks, axis=1).astype(jnp.int32)

    extra = jnp.maximum((seen.astype(jnp.int32) + (SLOTS - 1)) // SLOTS - 1, 0).astype(F32)
    sub = lax.broadcasted_iota(jnp.int32, (TILES, RIM), 0)
    lane = lax.broadcasted_iota(jnp.int32, (TILES, RIM), 1)
    extra_row = jnp.sum(jnp.where(sub == lane, extra, 0.0), axis=0, keepdims=True)
    extra_from = jnp.sum(jnp.where(lane < sub, extra_row, 0.0), axis=1, keepdims=True)
    extra_upto = extra_from + extra
    spill = jnp.sum(extra).astype(jnp.int32)
    spill_at = jnp.sum(member * extra_from, axis=0, keepdims=True).astype(jnp.int32)
    group = jnp.where(rank < SLOTS, tile, TILES + spill_at + rank // SLOTS - 1)
    group_hit = one_hot(GROUPS, group)
    slot_hit = ones_at(one_hot(SLOTS, rank % SLOTS))
    susc_high, susc_low = parts_of(as_row(susc_ref))
    features = (
        (from_local % RIM).astype(F32),
        ((as_row(to_ref) - base) % RIM).astype(F32),
        susc_high,
        susc_low,
    )
    table[...] = dot_last(
        jnp.concatenate([held_at(group_hit, value) for value in features], axis=0), slot_hit
    )

    def group_tile(at):
        rows = [table[pl.ds(part * GROUPS + at, 1), :] for part in range(4)]
        return tile_of_group(rows[0].astype(jnp.int32), rows[1].astype(jnp.int32), *rows[2:])

    for at in range(TILES):
        tiles[at] = group_tile(at)

    @pl.loop(0, spill)
    def _(step):
        passed = jnp.where(extra_upto <= step.astype(F32), 1.0, 0.0)
        owner = jnp.sum(passed).astype(jnp.int32)
        tiles[owner] = tiles[owner] + group_tile(TILES + step)

    rows = lax.broadcasted_iota(jnp.int32, (RIM, RIM), 0)
    cols = lax.broadcasted_iota(jnp.int32, (RIM, RIM), 1)
    zero = jnp.zeros((RIM, RIM), BF16)
    carried = jnp.zeros((1, RIM), F32)
    for at in range(TILES):
        pair, odd = at // 2, at % 2
        block = tiles[at]
        turned = block.T
        inside = jnp.where(cols > rows, block, jnp.where(cols < rows, turned, 0.0))
        ahead = jnp.where(cols > rows, 0.0, block)
        back = jnp.where(cols < rows, 0.0, turned)
        own = slice((1 + odd) * RIM, (2 + odd) * RIM)
        mine = slice(odd * RIM, (odd + 1) * RIM)
        other = slice((1 - odd) * RIM, (2 - odd) * RIM)
        for ref, kind in ((high_ref, 0), (low_ref, 1)):
            inside_part = split(inside)[kind]
            ahead_part = split(ahead)[kind]
            back_part = split(back)[kind]
            ref[pair, own, mine] = inside_part
            if odd == 0:
                ref[pair, 2 * RIM : 3 * RIM, mine] = back_part
                ref[pair, 3 * RIM :, mine] = zero
                ref[pair, RIM : 2 * RIM, other] = ahead_part
                if pair == 0:
                    ref[pair, :RIM, mine] = zero
            else:
                ref[pair, 3 * RIM :, mine] = back_part
                ref[pair, :RIM, mine] = zero
                if pair + 1 < PAIRS:
                    ref[pair + 1, :RIM, :RIM] = ahead_part
        degree_ref[:, at * RIM : (at + 1) * RIM] = (
            jnp.sum(inside, axis=0, keepdims=True)
            + jnp.sum(back, axis=0, keepdims=True)
            + carried
        )
        carried = jnp.sum(ahead, axis=0, keepdims=True)


def build_band(place, from_bus, to_bus, susceptance):
    shape = pltpu.VMEM((PAIRS, 4 * RIM, 2 * RIM), BF16)
    return pl.pallas_call(
        band_kernel,
        in_specs=[whole(pltpu.SMEM)] + [whole()] * 3,
        out_specs=[whole()] * 3,
        out_shape=[shape, shape, pltpu.VMEM((1, BUS_DEV), F32)],
        scratch_shapes=[
            pltpu.VMEM((TILES, RIM, RIM), F32),
            pltpu.VMEM((4 * GROUPS, SLOTS), F32),
        ],
        compiler_params=pltpu.CompilerParams(vmem_limit_bytes=VMEM_LIMIT),
        cost_estimate=pl.CostEstimate(flops=8 << 30, bytes_accessed=16 << 20, transcendentals=0),
        name="band",
    )(place, from_bus, to_bus, susceptance)


def outage_row(from_at, to_at, start, width):
    spots = lax.broadcasted_iota(jnp.int32, (1, width), 1) + start
    return jnp.where(spots == from_at, 1.0, 0.0) - jnp.where(spots == to_at, 1.0, 0.0)


def apply_pairs(halo, inner, stacks, high_ref, low_ref, cross, degrees, ends, susc, emit):
    flows = [jnp.zeros((PERIODS, RIM), F32) for _ in range(CASES)]
    for tile in range(-1, TILES + 1):
        value = halo(tile) if tile in (-1, TILES) else inner(tile * RIM, RIM)
        high, low = split(value)
        cols = slice((tile + 1) * RIM, (tile + 2) * RIM)
        stacks[:ROWS, cols] = high
        stacks[ROWS:, cols] = low
        for case in range(CASES):
            mask = outage_row(*ends[case], (tile + 1) * RIM, RIM)
            flows[case] += value[case * PERIODS : (case + 1) * PERIODS] * mask
    drops = [
        susc[case] * jnp.sum(flows[case], axis=1, keepdims=True) for case in range(CASES)
    ]
    width = 2 * RIM
    for pair in range(PAIRS):
        near = stacks[:, pair * width : pair * width + 2 * width]
        sums = dot_plain(near, high_ref[pair]) + dot_plain(near, low_ref[pair])
        sums = sums[:ROWS] + sums[ROWS:]
        if pair == 0:
            outer = dot_plain(stacks[:, :RIM], cross)
            outer = outer[:ROWS] + outer[ROWS:]
            outer = outer[:, :RIM] + outer[:, RIM:]
            sums = sums + jnp.concatenate([outer, jnp.zeros((ROWS, RIM), F32)], axis=1)
        cols = slice(pair * width, (pair + 1) * width)
        result = degrees(cols) * inner(pair * width, width) - sums
        parts = []
        for case in range(CASES):
            mask = outage_row(*ends[case], pair * width + RIM, width)
            parts.append(result[case * PERIODS : (case + 1) * PERIODS] - drops[case] * mask)
        emit(pair, cols, jnp.concatenate(parts, axis=0))


def resid_kernel(
    place_ref,
    outage_ref,
    field_ref,
    barrier_ref,
    high_ref,
    low_ref,
    own_degree_ref,
    from_ref,
    to_ref,
    susc_ref,
    left_ref,
    right_ref,
    dispatch_ref,
    gen_ref,
    weighted_ref,
    first_ref,
    last_ref,
    partial_ref,
    cross_ref,
    degree_ref,
    ends_ref,
    stacks,
    inject,
    total,
):
    block = place_ref[0]
    base = block * BUS_DEV
    keep = jnp.where(block > 0, 1.0, 0.0)
    left_rows = [
        jnp.concatenate(
            [left_ref[part * BR_ROWS + k : part * BR_ROWS + k + 1] for k in range(BR_ROWS)],
            axis=1,
        )
        for part in range(3)
    ]
    left_from = left_rows[0].astype(jnp.int32)
    left_to = left_rows[1].astype(jnp.int32)
    left_susc = left_rows[2] * keep
    high, low = parts_of(jnp.where(left_to >= base, left_susc, 0.0))
    hit = one_hot(RIM, (left_to - base) % RIM)
    left_ends = jnp.concatenate([held_at(hit, high), held_at(hit, low)], axis=0)
    both = dot_last(ones_at(one_hot(RIM, left_from - (base - RIM))), left_ends)
    across = both[:, :RIM] + both[:, RIM:]
    cross = jnp.concatenate(split(across), axis=1)
    cross_ref[...] = cross
    degree_ref[...] = own_degree_ref[...]
    degree_ref[:, :RIM] = own_degree_ref[:, :RIM] + jnp.sum(across, axis=0, keepdims=True)

    branch = lax.broadcasted_iota(jnp.int32, (1, BR_DEV), 1)
    own_rows = [as_row(from_ref).astype(F32), as_row(to_ref).astype(F32), as_row(susc_ref)]
    left_rows = [left_rows[0] * keep, left_rows[1] * keep, left_susc]
    ends, susc = [], []
    for case in range(CASES):
        own_hit = branch == outage_ref[case] - block * BR_DEV
        left_hit = branch == outage_ref[case] - (block - 1) * BR_DEV
        start, end, value = [
            jnp.sum(
                jnp.where(own_hit, own, 0.0) + jnp.where(left_hit, left, 0.0),
                axis=1,
                keepdims=True,
            )
            for own, left in zip(own_rows, left_rows)
        ]
        ends.append(
            (start.astype(jnp.int32) - base + RIM, end.astype(jnp.int32) - base + RIM)
        )
        susc.append(value)
        for k, held in enumerate((*ends[case], value)):
            at = 4 * k + case
            ends_ref[at : at + 1, :] = jnp.broadcast_to(held.astype(F32), (1, RIM))

    gen = as_row(gen_ref) - base
    gen_tile = gen // RIM
    gen_spots = ones_at(one_hot(RIM, gen % RIM))
    dispatch_parts = parts_of(dispatch_ref[...])
    share = TILES // 4
    for part in range(4):
        tiles = range(part * share, (part + 1) * share)
        picked = jnp.concatenate(
            [held_at(gen_tile == tile, value) for value in dispatch_parts for tile in tiles],
            axis=0,
        )
        spread = dot_last(picked, gen_spots)
        half = spread.shape[0] // 2
        inject[part * half : (part + 1) * half] = spread[:half] + spread[half:]

    def halo(tile):
        return left_ref[136:200] if tile < 0 else right_ref[...]

    def inner(start, width):
        return field_ref[:, start : start + width]

    def emit(pair, cols, result):
        rows = [slice((2 * pair + k) * PERIODS, (2 * pair + k + 1) * PERIODS) for k in (0, 1)]
        taken = jnp.concatenate([inject[rows[0]], inject[rows[1]]], axis=1)
        resid = result - jnp.concatenate([taken] * CASES, axis=0)
        weighted = barrier_ref[:, cols].astype(F32) * resid
        weighted_ref[:, cols] = weighted
        if pair == 0:
            first_ref[...] = weighted[:, :RIM]
        if pair == PAIRS - 1:
            last_ref[...] = weighted[:, RIM:]
        summed = weighted[0:16] + weighted[16:32] + (weighted[32:48] + weighted[48:64])
        total[rows[0]] = summed[:, :RIM]
        total[rows[1]] = summed[:, RIM:]

    def degrees(cols):
        return degree_ref[:, cols]

    apply_pairs(halo, inner, stacks, high_ref, low_ref, cross, degrees, ends, susc, emit)

    at_gens = jnp.zeros((PERIODS, G_DEV), F32)
    size = share * PERIODS
    for part in range(4):
        high, low = split(total[part * size : (part + 1) * size])
        both = dot_plain(jnp.concatenate([high, low], axis=0), gen_spots)
        for k in range(share):
            rows = slice(k * PERIODS, (k + 1) * PERIODS)
            value = both[rows] + both[size + k * PERIODS : size + (k + 1) * PERIODS]
            at_gens += jnp.where(gen_tile == part * share + k, value, 0.0)
    partial_ref[...] = at_gens


def residuals(place, outage, field, barrier, band, raw, halos, dispatch, gen_bus):
    tile = pltpu.VMEM((ROWS, RIM), F32)
    return pl.pallas_call(
        resid_kernel,
        in_specs=[whole(pltpu.SMEM)] * 2 + [whole()] * 12,
        out_specs=[whole()] * 7,
        out_shape=[
            pltpu.VMEM((ROWS, BUS_DEV), F32),
            tile,
            tile,
            pltpu.VMEM((PERIODS, G_DEV), F32),
            pltpu.VMEM((RIM, 2 * RIM), BF16),
            pltpu.VMEM((1, BUS_DEV), F32),
            pltpu.VMEM((16, RIM), F32),
        ],
        scratch_shapes=[
            pltpu.VMEM((2 * ROWS, BUS_DEV + 2 * RIM), BF16),
            pltpu.VMEM((TILES * PERIODS, RIM), F32),
            pltpu.VMEM((TILES * PERIODS, RIM), F32),
        ],
        compiler_params=pltpu.CompilerParams(vmem_limit_bytes=VMEM_LIMIT),
        cost_estimate=pl.CostEstimate(flops=4 << 30, bytes_accessed=8 << 20, transcendentals=0),
        name="resid",
    )(place, outage, field, barrier, *band, *raw, *halos, dispatch, gen_bus)


def angle_kernel(
    weighted_ref,
    field_ref,
    reg_ref,
    high_ref,
    low_ref,
    cross_ref,
    degree_ref,
    ends_ref,
    left_ref,
    right_ref,
    out_ref,
    stacks,
):
    ends, susc = [], []
    for case in range(CASES):
        held = [ends_ref[4 * k + case : 4 * k + case + 1, 0:1] for k in range(3)]
        ends.append((held[0].astype(jnp.int32), held[1].astype(jnp.int32)))
        susc.append(held[2])

    def halo(tile):
        return left_ref[...] if tile < 0 else right_ref[...]

    def inner(start, width):
        return weighted_ref[:, start : start + width]

    def emit(pair, cols, result):
        scale = jnp.concatenate([reg_ref[:, cols]] * CASES, axis=0)
        out_ref[:, cols] = result + scale * field_ref[:, cols]

    def degrees(cols):
        return degree_ref[:, cols]

    apply_pairs(
        halo, inner, stacks, high_ref, low_ref, cross_ref[...], degrees, ends, susc, emit
    )


def angles(weighted, field, reg, band, cross, degree, ends, halos):
    return pl.pallas_call(
        angle_kernel,
        in_specs=[whole()] * 10,
        out_specs=whole(),
        out_shape=jax.ShapeDtypeStruct((ROWS, BUS_DEV), F32),
        scratch_shapes=[pltpu.VMEM((2 * ROWS, BUS_DEV + 2 * RIM), BF16)],
        compiler_params=pltpu.CompilerParams(vmem_limit_bytes=VMEM_LIMIT),
        cost_estimate=pl.CostEstimate(flops=4 << 30, bytes_accessed=8 << 20, transcendentals=0),
        name="angles",
    )(weighted, field, reg, *band, cross, degree, ends, *halos)


def shifted(block, distance):
    size = lax.axis_size("net")
    return lax.ppermute(block, "net", [(i, (i + distance) % size) for i in range(size)])


def sum_cases(value):
    size = lax.axis_size("ctg")
    for mask in (1, 3, 4, 8, 16, 56):
        value = value + lax.ppermute(value, "ctg", [(i, i ^ mask) for i in range(size)])
    return value


def body(
    angle_dir,
    dispatch_dir,
    barrier,
    angle_reg,
    dispatch_reg,
    susceptance,
    from_bus,
    to_bus,
    outage,
    gen_bus,
):
    block = lax.axis_index("net")
    place = jnp.reshape(block, (1,)).astype(jnp.int32)
    field = angle_dir.reshape(ROWS, BUS_DEV)
    weights = barrier.reshape(ROWS, BUS_DEV)
    raw = (from_bus, to_bus, susceptance)
    packed, lead = pack(*raw, field)
    left = shifted(packed, 1)
    right = shifted(lead, -1)
    high, low, own_degree = build_band(place, *raw)
    weighted, first, last, partial, cross, degree, ends = residuals(
        place,
        outage,
        field,
        weights,
        (high, low, own_degree),
        raw,
        (left, right),
        dispatch_dir,
        gen_bus,
    )
    halos = (shifted(last, 1), shifted(first, -1))
    summed = sum_cases(partial)
    angle_out = angles(
        weighted, field, angle_reg, (high, low), cross, degree, ends, halos
    )
    case_count = float(CASES * lax.axis_size("ctg"))
    dispatch_out = dispatch_reg * dispatch_dir - summed / case_count
    return (angle_out.reshape(angle_dir.shape), dispatch_out)


def solution(mesh):
    placed = (
        P("ctg", None, "net"),
        P(None, "net"),
        P("ctg", None, "net"),
        P(None, "net"),
        P(None, "net"),
        P("net"),
        P("net"),
        P("net"),
        P("ctg"),
        P("net"),
    )
    return jax.shard_map(
        body,
        mesh=mesh,
        in_specs=placed,
        out_specs=(P("ctg", None, "net"), P(None, "net")),
        check_vma=False,
    )
```

```python
import jax
import jax.numpy as jnp
from jax import lax
from jax.experimental import pallas as pl
from jax.experimental.pallas import tpu as pltpu
from jax.sharding import PartitionSpec as P

BUS_DEV = 4096
BR_DEV = 5632
G_DEV = 1280
RIM = 128
PERIODS = 16
TILES = BUS_DEV // RIM
BR_ROWS = BR_DEV // RIM
PART_ROWS = 48
SENT_ROWS = 208
PAIRS = TILES // 2
CASES = 4
ROWS = CASES * PERIODS
VMEM_LIMIT = 20 * 1024 * 1024
SLOTS = 256
GROUPS = 64
WORK = 256
BF16 = jnp.bfloat16
F32 = jnp.float32


def split(value):
    high = value.astype(BF16)
    low = (value - high.astype(F32)).astype(BF16)
    return high, low


def dot_last(left, right):
    return lax.dot_general(
        left, right, (((1,), (1,)), ((), ())), preferred_element_type=F32
    )


def dot_plain(left, right):
    return jnp.dot(left, right, preferred_element_type=F32)


def whole(ref_space=pltpu.VMEM):
    return pl.BlockSpec(memory_space=ref_space)


def one_hot(rows, index):
    spots = lax.broadcasted_iota(jnp.int32, (rows, index.shape[1]), 0)
    return spots.astype(F32).astype(BF16) == index.astype(F32).astype(BF16)


def held_at(mask, values):
    return jnp.where(mask, values, jnp.zeros((), BF16))


def ones_at(mask):
    return held_at(mask, jnp.ones((), BF16))


def as_row(ref):
    return ref[...].reshape(1, ref.shape[0])


def pack_kernel(
    from_hbm, to_hbm, susc_hbm, field_hbm, out_ref, first_ref, from_ref, to_ref, susc_ref, sems
):
    moves = (
        (from_hbm, from_ref),
        (to_hbm, to_ref),
        (susc_hbm, susc_ref),
        (field_hbm.at[:, pl.ds(BUS_DEV - RIM, RIM)], out_ref.at[pl.ds(3 * PART_ROWS, ROWS), :]),
        (field_hbm.at[:, pl.ds(0, RIM)], first_ref),
    )
    copies = [pltpu.make_async_copy(*move, sems.at[k]) for k, move in enumerate(moves)]
    for copy in copies:
        copy.start()
    for part, ref in enumerate((from_ref, to_ref, susc_ref)):
        copies[part].wait()
        row = as_row(ref).astype(F32)
        for k in range(BR_ROWS):
            at = part * PART_ROWS + k
            out_ref[at : at + 1, :] = row[:, k * RIM : (k + 1) * RIM]
        out_ref[part * PART_ROWS + BR_ROWS : (part + 1) * PART_ROWS, :] = jnp.zeros(
            (PART_ROWS - BR_ROWS, RIM), F32
        )
    copies[3].wait()
    copies[4].wait()


def pack(from_bus, to_bus, susceptance, field):
    return pl.pallas_call(
        pack_kernel,
        in_specs=[whole(pltpu.HBM)] * 4,
        out_specs=[whole()] * 5,
        out_shape=[
            pltpu.VMEM((SENT_ROWS, RIM), F32),
            pltpu.VMEM((ROWS, RIM), F32),
            pltpu.VMEM((BR_DEV,), jnp.int32),
            pltpu.VMEM((BR_DEV,), jnp.int32),
            pltpu.VMEM((BR_DEV,), F32),
        ],
        scratch_shapes=[pltpu.SemaphoreType.DMA((5,))],
        compiler_params=pltpu.CompilerParams(vmem_limit_bytes=63 << 20),
        name="pack",
    )(from_bus, to_bus, susceptance, field)


def turned_tile(starts_row, to_row, high_row, low_row):
    starts = ones_at(one_hot(RIM, starts_row))
    hit = one_hot(RIM, to_row)
    high_row, low_row = high_row.astype(BF16), low_row.astype(BF16)
    ends = jnp.concatenate([held_at(hit, high_row), held_at(hit, low_row)], axis=0)
    both = dot_last(ends, starts)
    return both[:RIM] + both[RIM:]


def band_kernel(
    from_ref, to_ref, susc_ref, high_ref, low_ref, degree_ref, tiles, table
):
    base = lax.axis_index("net") * BUS_DEV
    from_local = as_row(from_ref) - base
    tile = from_local // RIM
    packed = ones_at(one_hot(TILES, tile))
    member = packed.astype(F32)
    chunks = BR_DEV // WORK
    rows = lax.broadcasted_iota(jnp.int32, (WORK, WORK), 0)
    cols = lax.broadcasted_iota(jnp.int32, (WORK, WORK), 1)
    upto = jnp.where(rows <= cols, 1.0, 0.0).astype(BF16)
    counts = dot_plain(
        jnp.concatenate([packed[:, c * WORK : (c + 1) * WORK] for c in range(chunks)], axis=0),
        upto,
    )
    seen = jnp.zeros((TILES, 1), F32)
    ranks = []
    for c in range(chunks):
        local = counts[c * TILES : (c + 1) * TILES]
        part = member[:, c * WORK : (c + 1) * WORK] * (local + seen)
        ranks.append(jnp.sum(part, axis=0, keepdims=True) - 1.0)
        seen = seen + local[:, WORK - 1 : WORK]
    rank = jnp.concatenate(ranks, axis=1).astype(jnp.int32)

    extra = jnp.maximum((seen.astype(jnp.int32) + (SLOTS - 1)) // SLOTS - 1, 0).astype(F32)
    sub = lax.broadcasted_iota(jnp.int32, (TILES, RIM), 0)
    lane = lax.broadcasted_iota(jnp.int32, (TILES, RIM), 1)
    extra_row = jnp.sum(jnp.where(sub == lane, extra, 0.0), axis=0, keepdims=True)
    extra_from = jnp.sum(jnp.where(lane < sub, extra_row, 0.0), axis=1, keepdims=True)
    extra_upto = extra_from + extra
    spill = jnp.sum(extra).astype(jnp.int32)
    spill_at = jnp.sum(member * extra_from, axis=0, keepdims=True).astype(jnp.int32)
    group = jnp.where(rank < SLOTS, tile, TILES + spill_at + rank // SLOTS - 1)
    group_hit = one_hot(GROUPS, group)
    slot_hit = ones_at(one_hot(SLOTS, rank % SLOTS))
    features = (
        (from_local % RIM).astype(F32).astype(BF16),
        ((as_row(to_ref) - base) % RIM).astype(F32).astype(BF16),
        *split(as_row(susc_ref)),
    )
    table[...] = dot_last(
        jnp.concatenate([held_at(group_hit, value) for value in features], axis=0), slot_hit
    )

    def group_tile(at):
        rows = [table[pl.ds(part * GROUPS + at, 1), :] for part in range(4)]
        return turned_tile(*rows)

    @pl.when(spill > 0)
    def _():
        tiles[...] = jnp.zeros_like(tiles)

        @pl.loop(0, spill)
        def _(step):
            passed = jnp.where(extra_upto <= step.astype(F32), 1.0, 0.0)
            owner = jnp.sum(passed).astype(jnp.int32)
            tiles[owner] = tiles[owner] + group_tile(TILES + step)

    rows = lax.broadcasted_iota(jnp.int32, (RIM, RIM), 0)
    cols = lax.broadcasted_iota(jnp.int32, (RIM, RIM), 1)
    later = cols > rows
    narrow = [x.astype(F32).astype(BF16) for x in (rows, cols)]
    above, below = narrow[1] > narrow[0], narrow[1] < narrow[0]
    zero = jnp.zeros((RIM, RIM), BF16)
    carried = jnp.zeros((1, RIM), F32)
    for at in range(TILES):
        pair, odd = at // 2, at % 2
        turned = group_tile(at) + jnp.where(spill > 0, tiles[at], 0.0)
        block = turned.T
        own = slice((1 + odd) * RIM, (2 + odd) * RIM)
        mine = slice(odd * RIM, (odd + 1) * RIM)
        other = slice((1 - odd) * RIM, (2 - odd) * RIM)
        for ref, part, back in zip((high_ref, low_ref), split(block), split(turned)):
            inside_part = jnp.where(above, part, jnp.where(below, back, zero))
            ahead_part = jnp.where(above, zero, part)
            back_part = jnp.where(below, zero, back)
            ref[pair, own, mine] = inside_part
            if odd == 0:
                ref[pair, 2 * RIM : 3 * RIM, mine] = back_part
                ref[pair, 3 * RIM :, mine] = zero
                ref[pair, RIM : 2 * RIM, other] = ahead_part
                if pair == 0:
                    ref[pair, :RIM, mine] = zero
            else:
                ref[pair, 3 * RIM :, mine] = back_part
                ref[pair, :RIM, mine] = zero
                if pair + 1 < PAIRS:
                    ref[pair + 1, :RIM, :RIM] = ahead_part
        inside = jnp.sum(jnp.where(later, block, 0.0), axis=0, keepdims=True)
        degree_ref[:, at * RIM : (at + 1) * RIM] = (
            inside + jnp.sum(turned, axis=0, keepdims=True) + carried
        )
        carried = jnp.sum(jnp.where(later, 0.0, block), axis=0, keepdims=True)


def build_band(from_bus, to_bus, susceptance):
    shape = pltpu.VMEM((PAIRS, 4 * RIM, 2 * RIM), BF16)
    return pl.pallas_call(
        band_kernel,
        in_specs=[whole()] * 3,
        out_specs=[whole()] * 3,
        out_shape=[shape, shape, pltpu.VMEM((1, BUS_DEV), F32)],
        scratch_shapes=[
            pltpu.VMEM((TILES, RIM, RIM), F32),
            pltpu.VMEM((4 * GROUPS, SLOTS), F32),
        ],
        compiler_params=pltpu.CompilerParams(vmem_limit_bytes=VMEM_LIMIT),
        cost_estimate=pl.CostEstimate(flops=8 << 30, bytes_accessed=16 << 20, transcendentals=0),
        name="band",
    )(from_bus, to_bus, susceptance)


def outage_row(from_at, to_at, start, width):
    spots = lax.broadcasted_iota(jnp.int32, (1, width), 1) + start
    return jnp.where(spots == from_at, 1.0, 0.0) - jnp.where(spots == to_at, 1.0, 0.0)


def apply_pairs(halo, inner, stacks, high_ref, low_ref, cross, degrees, ends, susc, emit):
    flows = [jnp.zeros((PERIODS, RIM), F32) for _ in range(CASES)]
    for tile in range(-1, TILES + 1):
        value = halo(tile) if tile in (-1, TILES) else inner(tile * RIM, RIM)
        high, low = split(value)
        cols = slice((tile + 1) * RIM, (tile + 2) * RIM)
        stacks[:ROWS, cols] = high
        stacks[ROWS:, cols] = low
        for case in range(CASES):
            mask = outage_row(*ends[case], (tile + 1) * RIM, RIM)
            flows[case] += value[case * PERIODS : (case + 1) * PERIODS] * mask
    drops = [
        susc[case] * jnp.sum(flows[case], axis=1, keepdims=True) for case in range(CASES)
    ]
    width = 2 * RIM
    for pair in range(PAIRS):
        near = stacks[:, pair * width : pair * width + 2 * width]
        sums = dot_plain(near, high_ref[pair]) + dot_plain(near, low_ref[pair])
        sums = sums[:ROWS] + sums[ROWS:]
        if pair == 0:
            outer = dot_plain(stacks[:, :RIM], cross)
            outer = outer[:ROWS] + outer[ROWS:]
            outer = outer[:, :RIM] + outer[:, RIM:]
            sums = sums + jnp.concatenate([outer, jnp.zeros((ROWS, RIM), F32)], axis=1)
        cols = slice(pair * width, (pair + 1) * width)
        result = degrees(cols) * inner(pair * width, width) - sums
        parts = []
        for case in range(CASES):
            mask = outage_row(*ends[case], pair * width + RIM, width)
            parts.append(result[case * PERIODS : (case + 1) * PERIODS] - drops[case] * mask)
        emit(pair, cols, jnp.concatenate(parts, axis=0))


def resid_kernel(
    outage_ref,
    field_ref,
    barrier_ref,
    high_ref,
    low_ref,
    own_degree_ref,
    own_ref,
    left_ref,
    right_ref,
    dispatch_ref,
    gen_ref,
    weighted_ref,
    first_ref,
    last_ref,
    partial_ref,
    cross_ref,
    degree_ref,
    ends_ref,
    stacks,
    inject,
    total,
):
    block = lax.axis_index("net")
    base = block * BUS_DEV
    keep = jnp.where(block > 0, 1.0, 0.0)
    shift = (base - RIM).astype(F32)
    starts, stops, values = [
        left_ref[part * PART_ROWS : (part + 1) * PART_ROWS] for part in range(3)
    ]
    starts, stops, values = starts - shift, stops - shift, values * keep
    crossing = stops >= RIM
    from_row, to_row, high_row, low_row = [
        jnp.concatenate([part[k : k + 1] for k in range(BR_ROWS)], axis=1)
        for part in (
            starts,
            stops - RIM,
            *[part.astype(F32) for part in split(jnp.where(crossing, values, 0.0))],
        )
    ]
    hit = one_hot(RIM, to_row)
    left_ends = jnp.concatenate(
        [held_at(hit, high_row.astype(BF16)), held_at(hit, low_row.astype(BF16))], axis=0
    )
    both = dot_last(ones_at(one_hot(RIM, from_row)), left_ends)
    across = both[:, :RIM] + both[:, RIM:]
    cross = jnp.concatenate(split(across), axis=1)
    cross_ref[...] = cross
    degree_ref[...] = own_degree_ref[...]
    degree_ref[:, :RIM] = own_degree_ref[:, :RIM] + jnp.sum(across, axis=0, keepdims=True)

    own_starts, own_stops, own_values = [
        own_ref[part * PART_ROWS : (part + 1) * PART_ROWS] for part in range(3)
    ]
    pairs = (
        (own_starts - shift, starts * keep),
        (own_stops - shift, stops * keep),
        (own_values, values),
    )
    branch = (
        lax.broadcasted_iota(jnp.int32, (PART_ROWS, RIM), 0) * RIM
        + lax.broadcasted_iota(jnp.int32, (PART_ROWS, RIM), 1)
        + block * BR_DEV
    )
    inside = lax.broadcasted_iota(jnp.int32, (PART_ROWS, RIM), 0) < BR_ROWS
    branch = jnp.where(inside, branch, -BR_DEV - 1)
    out_row = outage_ref[...].reshape(1, CASES)
    ends, susc = [], []
    for case in range(CASES):
        out = out_row[:, case : case + 1]
        own_hit = branch == out
        left_hit = branch == out + BR_DEV
        start, end, value = [
            jnp.sum(
                jnp.sum(
                    jnp.where(own_hit, own, 0.0) + jnp.where(left_hit, left, 0.0),
                    axis=0,
                    keepdims=True,
                ),
                axis=1,
                keepdims=True,
            )
            for own, left in pairs
        ]
        ends.append((start.astype(jnp.int32), end.astype(jnp.int32)))
        susc.append(value)
        for k, held in enumerate((start, end, value)):
            at = 4 * k + case
            ends_ref[at : at + 1, :] = jnp.broadcast_to(held, (1, RIM))

    gen = as_row(gen_ref) - base
    gen_tile = gen // RIM
    gen_hits = [gen_tile.astype(F32).astype(BF16) == tile for tile in range(TILES)]
    gen_spots = ones_at(one_hot(RIM, gen % RIM))
    dispatch_parts = split(dispatch_ref[...])
    share = TILES // 4
    for part in range(4):
        tiles = range(part * share, (part + 1) * share)
        picked = jnp.concatenate(
            [held_at(gen_hits[tile], value) for value in dispatch_parts for tile in tiles],
            axis=0,
        )
        spread = dot_last(picked, gen_spots)
        half = spread.shape[0] // 2
        inject[part * half : (part + 1) * half] = spread[:half] + spread[half:]

    def halo(tile):
        return left_ref[3 * PART_ROWS :] if tile < 0 else right_ref[...]

    def inner(start, width):
        return field_ref[:, start : start + width]

    def emit(pair, cols, result):
        rows = [slice((2 * pair + k) * PERIODS, (2 * pair + k + 1) * PERIODS) for k in (0, 1)]
        taken = jnp.concatenate([inject[rows[0]], inject[rows[1]]], axis=1)
        resid = result - jnp.concatenate([taken] * CASES, axis=0)
        weighted = barrier_ref[:, cols].astype(F32) * resid
        weighted_ref[:, cols] = weighted
        if pair == 0:
            first_ref[...] = weighted[:, :RIM]
        if pair == PAIRS - 1:
            last_ref[...] = weighted[:, RIM:]
        summed = weighted[0:16] + weighted[16:32] + (weighted[32:48] + weighted[48:64])
        total[rows[0]] = summed[:, :RIM]
        total[rows[1]] = summed[:, RIM:]

    def degrees(cols):
        return degree_ref[:, cols]

    apply_pairs(halo, inner, stacks, high_ref, low_ref, cross, degrees, ends, susc, emit)

    at_gens = jnp.zeros((PERIODS, G_DEV), F32)
    size = share * PERIODS
    for part in range(4):
        high, low = split(total[part * size : (part + 1) * size])
        both = dot_plain(jnp.concatenate([high, low], axis=0), gen_spots)
        for k in range(share):
            rows = slice(k * PERIODS, (k + 1) * PERIODS)
            value = both[rows] + both[size + k * PERIODS : size + (k + 1) * PERIODS]
            at_gens += jnp.where(gen_tile == part * share + k, value, 0.0)
    partial_ref[...] = at_gens


def residuals(outage, field, barrier, band, own, halos, dispatch, gen_bus):
    tile = pltpu.VMEM((ROWS, RIM), F32)
    return pl.pallas_call(
        resid_kernel,
        in_specs=[whole()] * 11,
        out_specs=[whole()] * 7,
        out_shape=[
            pltpu.VMEM((ROWS, BUS_DEV), F32),
            tile,
            tile,
            pltpu.VMEM((PERIODS, G_DEV), F32),
            pltpu.VMEM((RIM, 2 * RIM), BF16),
            pltpu.VMEM((1, BUS_DEV), F32),
            pltpu.VMEM((16, RIM), F32),
        ],
        scratch_shapes=[
            pltpu.VMEM((2 * ROWS, BUS_DEV + 2 * RIM), BF16),
            pltpu.VMEM((TILES * PERIODS, RIM), F32),
            pltpu.VMEM((TILES * PERIODS, RIM), F32),
        ],
        compiler_params=pltpu.CompilerParams(vmem_limit_bytes=VMEM_LIMIT),
        cost_estimate=pl.CostEstimate(flops=4 << 30, bytes_accessed=8 << 20, transcendentals=0),
        name="resid",
    )(outage, field, barrier, *band, own, *halos, dispatch, gen_bus)


def angle_kernel(
    weighted_ref,
    field_ref,
    reg_ref,
    high_ref,
    low_ref,
    cross_ref,
    degree_ref,
    ends_ref,
    left_ref,
    right_ref,
    out_ref,
    stacks,
):
    ends, susc = [], []
    for case in range(CASES):
        held = [ends_ref[4 * k + case : 4 * k + case + 1, 0:1] for k in range(3)]
        ends.append((held[0].astype(jnp.int32), held[1].astype(jnp.int32)))
        susc.append(held[2])

    def halo(tile):
        return left_ref[...] if tile < 0 else right_ref[...]

    def inner(start, width):
        return weighted_ref[:, start : start + width]

    def emit(pair, cols, result):
        scale = jnp.concatenate([reg_ref[:, cols]] * CASES, axis=0)
        out_ref[:, cols] = result + scale * field_ref[:, cols]

    def degrees(cols):
        return degree_ref[:, cols]

    apply_pairs(
        halo, inner, stacks, high_ref, low_ref, cross_ref[...], degrees, ends, susc, emit
    )


def angles(weighted, field, reg, band, cross, degree, ends, halos):
    return pl.pallas_call(
        angle_kernel,
        in_specs=[whole()] * 10,
        out_specs=whole(),
        out_shape=jax.ShapeDtypeStruct((ROWS, BUS_DEV), F32),
        scratch_shapes=[pltpu.VMEM((2 * ROWS, BUS_DEV + 2 * RIM), BF16)],
        compiler_params=pltpu.CompilerParams(vmem_limit_bytes=VMEM_LIMIT),
        cost_estimate=pl.CostEstimate(flops=4 << 30, bytes_accessed=8 << 20, transcendentals=0),
        name="angles",
    )(weighted, field, reg, *band, cross, degree, ends, *halos)


def shifted(block, distance):
    size = lax.axis_size("net")
    return lax.ppermute(block, "net", [(i, (i + distance) % size) for i in range(size)])


def sum_cases(value):
    size = lax.axis_size("ctg")
    for masks in ((8,), (16,), (1, 2, 3), (4,), (40,)):
        parts = [
            lax.ppermute(value, "ctg", [(i, i ^ mask) for i in range(size)]) for mask in masks
        ]
        for part in parts:
            value = value + part
    return value


def body(
    angle_dir,
    dispatch_dir,
    barrier,
    angle_reg,
    dispatch_reg,
    susceptance,
    from_bus,
    to_bus,
    outage,
    gen_bus,
):
    field = angle_dir.reshape(ROWS, BUS_DEV)
    weights = barrier.reshape(ROWS, BUS_DEV)
    packed, lead, *raw = pack(from_bus, to_bus, susceptance, field)
    left = shifted(packed, 1)
    right = shifted(lead, -1)
    high, low, own_degree = build_band(*raw)
    weighted, first, last, partial, cross, degree, ends = residuals(
        outage,
        field,
        weights,
        (high, low, own_degree),
        packed,
        (left, right),
        dispatch_dir,
        gen_bus,
    )
    halos = (shifted(last, 1), shifted(first, -1))
    summed = sum_cases(partial)
    angle_out = angles(
        weighted, field, angle_reg, (high, low), cross, degree, ends, halos
    )
    case_count = float(CASES * lax.axis_size("ctg"))
    dispatch_out = dispatch_reg * dispatch_dir - summed / case_count
    return (angle_out.reshape(angle_dir.shape), dispatch_out)


def solution(mesh):
    placed = (
        P("ctg", None, "net"),
        P(None, "net"),
        P("ctg", None, "net"),
        P(None, "net"),
        P(None, "net"),
        P("net"),
        P("net"),
        P("net"),
        P("ctg"),
        P("net"),
    )
    return jax.shard_map(
        body,
        mesh=mesh,
        in_specs=placed,
        out_specs=(P("ctg", None, "net"), P(None, "net")),
        check_vma=False,
    )
```

```python
import jax
import jax.numpy as jnp
from jax import lax
from jax.experimental import pallas as pl
from jax.experimental.pallas import tpu as pltpu
from jax.sharding import PartitionSpec as P

BUS_DEV = 4096
BR_DEV = 5632
G_DEV = 1280
RIM = 128
PERIODS = 16
TILES = BUS_DEV // RIM
BR_ROWS = BR_DEV // RIM
PART_ROWS = 48
SENT_ROWS = 208
PAIRS = TILES // 2
CASES = 4
ROWS = CASES * PERIODS
VMEM_LIMIT = 20 * 1024 * 1024
WIDE = 2 * RIM
SLOTS = 256
GROUPS = 64
WORK = 256
BF16 = jnp.bfloat16
F32 = jnp.float32


def split(value):
    high = value.astype(BF16)
    low = (value - high.astype(F32)).astype(BF16)
    return high, low


def dot_last(left, right):
    return lax.dot_general(
        left, right, (((1,), (1,)), ((), ())), preferred_element_type=F32
    )


def dot_plain(left, right):
    return jnp.dot(left, right, preferred_element_type=F32)


def whole(ref_space=pltpu.VMEM):
    return pl.BlockSpec(memory_space=ref_space)


def one_hot(rows, index):
    spots = lax.broadcasted_iota(jnp.int32, (rows, index.shape[1]), 0)
    return spots.astype(F32).astype(BF16) == index.astype(F32).astype(BF16)


def one_hot_turned(index, columns):
    spots = lax.broadcasted_iota(jnp.int32, (index.shape[0], columns), 1)
    return spots.astype(F32).astype(BF16) == index.astype(BF16)


def held_at(mask, values):
    return jnp.where(mask, values, jnp.zeros((), BF16))


def ones_at(mask):
    return held_at(mask, jnp.ones((), BF16))


def as_row(ref):
    return ref[...].reshape(1, ref.shape[0])


def pack_kernel(
    from_hbm, to_hbm, susc_hbm, field_hbm, out_ref, first_ref, from_ref, to_ref, susc_ref, sems
):
    moves = (
        (from_hbm, from_ref),
        (to_hbm, to_ref),
        (susc_hbm, susc_ref),
        (field_hbm.at[:, pl.ds(BUS_DEV - RIM, RIM)], out_ref.at[pl.ds(3 * PART_ROWS, ROWS), :]),
        (field_hbm.at[:, pl.ds(0, RIM)], first_ref),
    )
    copies = [pltpu.make_async_copy(*move, sems.at[k]) for k, move in enumerate(moves)]
    for copy in copies:
        copy.start()
    for part, ref in enumerate((from_ref, to_ref, susc_ref)):
        copies[part].wait()
        row = as_row(ref).astype(F32)
        for k in range(BR_ROWS):
            at = part * PART_ROWS + k
            out_ref[at : at + 1, :] = row[:, k * RIM : (k + 1) * RIM]
        out_ref[part * PART_ROWS + BR_ROWS : (part + 1) * PART_ROWS, :] = jnp.zeros(
            (PART_ROWS - BR_ROWS, RIM), F32
        )
    copies[3].wait()
    copies[4].wait()


def pack(from_bus, to_bus, susceptance, field):
    return pl.pallas_call(
        pack_kernel,
        in_specs=[whole(pltpu.HBM)] * 4,
        out_specs=[whole()] * 5,
        out_shape=[
            pltpu.VMEM((SENT_ROWS, RIM), F32),
            pltpu.VMEM((ROWS, RIM), F32),
            pltpu.VMEM((BR_DEV,), jnp.int32),
            pltpu.VMEM((BR_DEV,), jnp.int32),
            pltpu.VMEM((BR_DEV,), F32),
        ],
        scratch_shapes=[pltpu.SemaphoreType.DMA((5,))],
        compiler_params=pltpu.CompilerParams(vmem_limit_bytes=63 << 20),
        name="pack",
    )(from_bus, to_bus, susceptance, field)


def turned_tile(starts_row, to_row, high_row, low_row):
    starts = ones_at(one_hot(RIM, starts_row))
    hit = one_hot(RIM, to_row)
    high_row, low_row = high_row.astype(BF16), low_row.astype(BF16)
    ends = jnp.concatenate([held_at(hit, high_row), held_at(hit, low_row)], axis=0)
    both = dot_last(ends, starts)
    return both[:RIM] + both[RIM:]


def band_kernel(
    from_ref, to_ref, susc_ref, high_ref, low_ref, degree_ref, tiles, table
):
    base = lax.axis_index("net") * BUS_DEV
    from_local = as_row(from_ref) - base
    tile = from_local // RIM
    packed = ones_at(one_hot(TILES, tile))
    member = packed.astype(F32)
    chunks = BR_DEV // WORK
    rows = lax.broadcasted_iota(jnp.int32, (WORK, WORK), 0)
    cols = lax.broadcasted_iota(jnp.int32, (WORK, WORK), 1)
    upto = jnp.where(rows <= cols, 1.0, 0.0).astype(BF16)
    counts = dot_plain(
        jnp.concatenate([packed[:, c * WORK : (c + 1) * WORK] for c in range(chunks)], axis=0),
        upto,
    )
    seen = jnp.zeros((TILES, 1), F32)
    ranks = []
    for c in range(chunks):
        local = counts[c * TILES : (c + 1) * TILES]
        part = member[:, c * WORK : (c + 1) * WORK] * (local + seen)
        ranks.append(jnp.sum(part, axis=0, keepdims=True) - 1.0)
        seen = seen + local[:, WORK - 1 : WORK]
    rank = jnp.concatenate(ranks, axis=1).astype(jnp.int32)

    extra = jnp.maximum((seen.astype(jnp.int32) + (SLOTS - 1)) // SLOTS - 1, 0).astype(F32)
    sub = lax.broadcasted_iota(jnp.int32, (TILES, RIM), 0)
    lane = lax.broadcasted_iota(jnp.int32, (TILES, RIM), 1)
    extra_row = jnp.sum(jnp.where(sub == lane, extra, 0.0), axis=0, keepdims=True)
    extra_from = jnp.sum(jnp.where(lane < sub, extra_row, 0.0), axis=1, keepdims=True)
    extra_upto = extra_from + extra
    spill = jnp.sum(extra).astype(jnp.int32)
    spill_at = jnp.sum(member * extra_from, axis=0, keepdims=True).astype(jnp.int32)
    group = jnp.where(rank < SLOTS, tile, TILES + spill_at + rank // SLOTS - 1)
    group_hit = one_hot(GROUPS, group)
    slot_hit = ones_at(one_hot(SLOTS, rank % SLOTS))
    features = (
        (from_local % RIM).astype(F32).astype(BF16),
        ((as_row(to_ref) - base) % RIM).astype(F32).astype(BF16),
        *split(as_row(susc_ref)),
    )
    table[...] = dot_last(
        jnp.concatenate([held_at(group_hit, value) for value in features], axis=0), slot_hit
    )

    def group_tile(at):
        rows = [table[pl.ds(part * GROUPS + at, 1), :] for part in range(4)]
        return turned_tile(*rows)

    @pl.when(spill > 0)
    def _():
        tiles[...] = jnp.zeros_like(tiles)

        @pl.loop(0, spill)
        def _(step):
            passed = jnp.where(extra_upto <= step.astype(F32), 1.0, 0.0)
            owner = jnp.sum(passed).astype(jnp.int32)
            tiles[owner] = tiles[owner] + group_tile(TILES + step)

    rows = lax.broadcasted_iota(jnp.int32, (RIM, RIM), 0)
    cols = lax.broadcasted_iota(jnp.int32, (RIM, RIM), 1)
    later = cols > rows
    narrow = [x.astype(F32).astype(BF16) for x in (rows, cols)]
    above, below = narrow[1] > narrow[0], narrow[1] < narrow[0]
    zero = jnp.zeros((RIM, RIM), BF16)
    carried = jnp.zeros((1, RIM), F32)
    for at in range(TILES):
        pair, odd = at // 2, at % 2
        turned = group_tile(at) + jnp.where(spill > 0, tiles[at], 0.0)
        block = turned.T
        own = slice((1 + odd) * RIM, (2 + odd) * RIM)
        mine = slice(odd * RIM, (odd + 1) * RIM)
        other = slice((1 - odd) * RIM, (2 - odd) * RIM)
        for ref, part, back in zip((high_ref, low_ref), split(block), split(turned)):
            inside_part = jnp.where(above, part, jnp.where(below, back, zero))
            ahead_part = jnp.where(above, zero, part)
            back_part = jnp.where(below, zero, back)
            ref[pair, own, mine] = inside_part
            if odd == 0:
                ref[pair, 2 * RIM : 3 * RIM, mine] = back_part
                ref[pair, 3 * RIM :, mine] = zero
                ref[pair, RIM : 2 * RIM, other] = ahead_part
                if pair == 0:
                    ref[pair, :RIM, mine] = zero
            else:
                ref[pair, 3 * RIM :, mine] = back_part
                ref[pair, :RIM, mine] = zero
                if pair + 1 < PAIRS:
                    ref[pair + 1, :RIM, :RIM] = ahead_part
        inside = jnp.sum(jnp.where(later, block, 0.0), axis=0, keepdims=True)
        degree_ref[:, at * RIM : (at + 1) * RIM] = (
            inside + jnp.sum(turned, axis=0, keepdims=True) + carried
        )
        carried = jnp.sum(jnp.where(later, 0.0, block), axis=0, keepdims=True)


def build_band(from_bus, to_bus, susceptance):
    shape = pltpu.VMEM((PAIRS, 4 * RIM, 2 * RIM), BF16)
    return pl.pallas_call(
        band_kernel,
        in_specs=[whole()] * 3,
        out_specs=[whole()] * 3,
        out_shape=[shape, shape, pltpu.VMEM((1, BUS_DEV), F32)],
        scratch_shapes=[
            pltpu.VMEM((TILES, RIM, RIM), F32),
            pltpu.VMEM((4 * GROUPS, SLOTS), F32),
        ],
        compiler_params=pltpu.CompilerParams(vmem_limit_bytes=VMEM_LIMIT),
        cost_estimate=pl.CostEstimate(flops=8 << 30, bytes_accessed=16 << 20, transcendentals=0),
        name="band",
    )(from_bus, to_bus, susceptance)


def outage_row(from_at, to_at, start, width):
    spots = lax.broadcasted_iota(jnp.int32, (1, width), 1) + start
    return jnp.where(spots == from_at, 1.0, 0.0) - jnp.where(spots == to_at, 1.0, 0.0)


def apply_pairs(halo, inner, stacks, high_ref, low_ref, cross, degrees, ends, susc, emit):
    flows = [jnp.zeros((PERIODS, RIM), F32) for _ in range(CASES)]
    for tile in range(-1, TILES + 1):
        value = halo(tile) if tile in (-1, TILES) else inner(tile * RIM, RIM)
        high, low = split(value)
        cols = slice((tile + 1) * RIM, (tile + 2) * RIM)
        stacks[:ROWS, cols] = high
        stacks[ROWS:, cols] = low
        for case in range(CASES):
            mask = outage_row(*ends[case], (tile + 1) * RIM, RIM)
            flows[case] += value[case * PERIODS : (case + 1) * PERIODS] * mask
    drops = [
        susc[case] * jnp.sum(flows[case], axis=1, keepdims=True) for case in range(CASES)
    ]
    width = 2 * RIM
    for pair in range(PAIRS):
        near = stacks[:, pair * width : pair * width + 2 * width]
        sums = dot_plain(near, high_ref[pair]) + dot_plain(near, low_ref[pair])
        sums = sums[:ROWS] + sums[ROWS:]
        if pair == 0:
            outer = dot_plain(stacks[:, :RIM], cross)
            outer = outer[:ROWS] + outer[ROWS:]
            outer = outer[:, :RIM] + outer[:, RIM:]
            sums = sums + jnp.concatenate([outer, jnp.zeros((ROWS, RIM), F32)], axis=1)
        cols = slice(pair * width, (pair + 1) * width)
        result = degrees(cols) * inner(pair * width, width) - sums
        parts = []
        for case in range(CASES):
            mask = outage_row(*ends[case], pair * width + RIM, width)
            parts.append(result[case * PERIODS : (case + 1) * PERIODS] - drops[case] * mask)
        emit(pair, cols, jnp.concatenate(parts, axis=0))


def resid_kernel(
    outage_ref,
    field_ref,
    barrier_ref,
    high_ref,
    low_ref,
    own_degree_ref,
    own_ref,
    left_ref,
    right_ref,
    dispatch_ref,
    gen_ref,
    weighted_ref,
    first_ref,
    last_ref,
    partial_ref,
    cross_ref,
    degree_ref,
    ends_ref,
    stacks,
    inject,
    total,
):
    block = lax.axis_index("net")
    base = block * BUS_DEV
    keep = jnp.where(block > 0, 1.0, 0.0)
    shift = (base - RIM).astype(F32)
    starts, stops, values = [
        left_ref[part * PART_ROWS : (part + 1) * PART_ROWS] for part in range(3)
    ]
    starts, stops, values = starts - shift, stops - shift, values * keep
    crossing = stops >= RIM
    from_row, to_row, high_row, low_row = [
        jnp.concatenate([part[k : k + 1] for k in range(BR_ROWS)], axis=1)
        for part in (
            starts,
            stops - RIM,
            *[part.astype(F32) for part in split(jnp.where(crossing, values, 0.0))],
        )
    ]
    hit = one_hot(RIM, to_row)
    left_ends = jnp.concatenate(
        [held_at(hit, high_row.astype(BF16)), held_at(hit, low_row.astype(BF16))], axis=0
    )
    columns = starts.T
    turned_starts = jnp.concatenate(
        [ones_at(one_hot_turned(columns[:, k : k + 1], RIM)) for k in range(BR_ROWS)],
        axis=0,
    )
    both = dot_plain(left_ends, turned_starts)
    across = (both[:RIM] + both[RIM:]).T
    cross = jnp.concatenate(split(across), axis=1)
    cross_ref[...] = cross
    degree_ref[...] = own_degree_ref[...]
    degree_ref[:, :RIM] = own_degree_ref[:, :RIM] + jnp.sum(across, axis=0, keepdims=True)

    own_starts, own_stops, own_values = [
        own_ref[part * PART_ROWS : (part + 1) * PART_ROWS] for part in range(3)
    ]
    pairs = (
        (own_starts - shift, starts * keep),
        (own_stops - shift, stops * keep),
        (own_values, values),
    )
    branch = (
        lax.broadcasted_iota(jnp.int32, (PART_ROWS, RIM), 0) * RIM
        + lax.broadcasted_iota(jnp.int32, (PART_ROWS, RIM), 1)
        + block * BR_DEV
    )
    inside = lax.broadcasted_iota(jnp.int32, (PART_ROWS, RIM), 0) < BR_ROWS
    branch = jnp.where(inside, branch, -BR_DEV - 1)
    out_row = outage_ref[...].reshape(1, CASES)
    ends, susc = [], []
    for case in range(CASES):
        out = out_row[:, case : case + 1]
        own_hit = branch == out
        left_hit = branch == out + BR_DEV
        start, end, value = [
            jnp.sum(
                jnp.sum(
                    jnp.where(own_hit, own, 0.0) + jnp.where(left_hit, left, 0.0),
                    axis=0,
                    keepdims=True,
                ),
                axis=1,
                keepdims=True,
            )
            for own, left in pairs
        ]
        ends.append((start.astype(jnp.int32), end.astype(jnp.int32)))
        susc.append(value)
        for k, held in enumerate((start, end, value)):
            at = 4 * k + case
            ends_ref[at : at + 1, :] = jnp.broadcast_to(held, (1, RIM))

    gen = as_row(gen_ref) - base
    gen_pair = gen // WIDE
    gen_hits = [gen_pair.astype(F32).astype(BF16) == pair for pair in range(PAIRS)]
    gen_spots = ones_at(one_hot(WIDE, gen % WIDE))
    picked = jnp.concatenate(
        [held_at(hit, value) for value in split(dispatch_ref[...]) for hit in gen_hits], axis=0
    )
    spread = dot_last(picked, gen_spots)
    inject[...] = spread[: PAIRS * PERIODS] + spread[PAIRS * PERIODS :]

    def halo(tile):
        return left_ref[3 * PART_ROWS :] if tile < 0 else right_ref[...]

    def inner(start, width):
        return field_ref[:, start : start + width]

    def emit(pair, cols, result):
        rows = slice(pair * PERIODS, (pair + 1) * PERIODS)
        taken = inject[rows]
        resid = result - jnp.concatenate([taken] * CASES, axis=0)
        weighted = barrier_ref[:, cols].astype(F32) * resid
        weighted_ref[:, cols] = weighted
        if pair == 0:
            first_ref[...] = weighted[:, :RIM]
        if pair == PAIRS - 1:
            last_ref[...] = weighted[:, RIM:]
        total[rows] = (
            weighted[0:16] + weighted[16:32] + (weighted[32:48] + weighted[48:64])
        )

    def degrees(cols):
        return degree_ref[:, cols]

    apply_pairs(halo, inner, stacks, high_ref, low_ref, cross, degrees, ends, susc, emit)

    at_gens = jnp.zeros((PERIODS, G_DEV), F32)
    size = PAIRS * PERIODS // 2
    for part in range(2):
        high, low = split(total[part * size : (part + 1) * size])
        both = dot_plain(jnp.concatenate([high, low], axis=0), gen_spots)
        for k in range(PAIRS // 2):
            rows = slice(k * PERIODS, (k + 1) * PERIODS)
            value = both[rows] + both[size + k * PERIODS : size + (k + 1) * PERIODS]
            at_gens += jnp.where(gen_pair == part * (PAIRS // 2) + k, value, 0.0)
    partial_ref[...] = at_gens


def residuals(outage, field, barrier, band, own, halos, dispatch, gen_bus):
    tile = pltpu.VMEM((ROWS, RIM), F32)
    return pl.pallas_call(
        resid_kernel,
        in_specs=[whole()] * 11,
        out_specs=[whole()] * 7,
        out_shape=[
            pltpu.VMEM((ROWS, BUS_DEV), F32),
            tile,
            tile,
            pltpu.VMEM((PERIODS, G_DEV), F32),
            pltpu.VMEM((RIM, 2 * RIM), BF16),
            pltpu.VMEM((1, BUS_DEV), F32),
            pltpu.VMEM((16, RIM), F32),
        ],
        scratch_shapes=[
            pltpu.VMEM((2 * ROWS, BUS_DEV + 2 * RIM), BF16),
            pltpu.VMEM((PAIRS * PERIODS, WIDE), F32),
            pltpu.VMEM((PAIRS * PERIODS, WIDE), F32),
        ],
        compiler_params=pltpu.CompilerParams(vmem_limit_bytes=VMEM_LIMIT),
        cost_estimate=pl.CostEstimate(flops=4 << 30, bytes_accessed=8 << 20, transcendentals=0),
        name="resid",
    )(outage, field, barrier, *band, own, *halos, dispatch, gen_bus)


def angle_kernel(
    weighted_ref,
    field_ref,
    reg_ref,
    high_ref,
    low_ref,
    cross_ref,
    degree_ref,
    ends_ref,
    left_ref,
    right_ref,
    out_ref,
    stacks,
):
    ends, susc = [], []
    for case in range(CASES):
        held = [ends_ref[4 * k + case : 4 * k + case + 1, 0:1] for k in range(3)]
        ends.append((held[0].astype(jnp.int32), held[1].astype(jnp.int32)))
        susc.append(held[2])

    def halo(tile):
        return left_ref[...] if tile < 0 else right_ref[...]

    def inner(start, width):
        return weighted_ref[:, start : start + width]

    def emit(pair, cols, result):
        scale = jnp.concatenate([reg_ref[:, cols]] * CASES, axis=0)
        out_ref[:, cols] = result + scale * field_ref[:, cols]

    def degrees(cols):
        return degree_ref[:, cols]

    apply_pairs(
        halo, inner, stacks, high_ref, low_ref, cross_ref[...], degrees, ends, susc, emit
    )


def angles(weighted, field, reg, band, cross, degree, ends, halos):
    return pl.pallas_call(
        angle_kernel,
        in_specs=[whole()] * 10,
        out_specs=whole(),
        out_shape=jax.ShapeDtypeStruct((ROWS, BUS_DEV), F32),
        scratch_shapes=[pltpu.VMEM((2 * ROWS, BUS_DEV + 2 * RIM), BF16)],
        compiler_params=pltpu.CompilerParams(vmem_limit_bytes=VMEM_LIMIT),
        cost_estimate=pl.CostEstimate(flops=4 << 30, bytes_accessed=8 << 20, transcendentals=0),
        name="angles",
    )(weighted, field, reg, *band, cross, degree, ends, *halos)


def shifted(block, distance):
    size = lax.axis_size("net")
    return lax.ppermute(block, "net", [(i, (i + distance) % size) for i in range(size)])


def sum_cases(value):
    size = lax.axis_size("ctg")
    for masks in ((8,), (16,), (1, 2, 3), (4,), (40,)):
        parts = [
            lax.ppermute(value, "ctg", [(i, i ^ mask) for i in range(size)]) for mask in masks
        ]
        for part in parts:
            value = value + part
    return value


def body(
    angle_dir,
    dispatch_dir,
    barrier,
    angle_reg,
    dispatch_reg,
    susceptance,
    from_bus,
    to_bus,
    outage,
    gen_bus,
):
    field = angle_dir.reshape(ROWS, BUS_DEV)
    weights = barrier.reshape(ROWS, BUS_DEV)
    packed, lead, *raw = pack(from_bus, to_bus, susceptance, field)
    left = shifted(packed, 1)
    right = shifted(lead, -1)
    high, low, own_degree = build_band(*raw)
    weighted, first, last, partial, cross, degree, ends = residuals(
        outage,
        field,
        weights,
        (high, low, own_degree),
        packed,
        (left, right),
        dispatch_dir,
        gen_bus,
    )
    halos = (shifted(last, 1), shifted(first, -1))
    summed = sum_cases(partial)
    angle_out = angles(
        weighted, field, angle_reg, (high, low), cross, degree, ends, halos
    )
    case_count = float(CASES * lax.axis_size("ctg"))
    dispatch_out = dispatch_reg * dispatch_dir - summed / case_count
    return (angle_out.reshape(angle_dir.shape), dispatch_out)


def solution(mesh):
    placed = (
        P("ctg", None, "net"),
        P(None, "net"),
        P("ctg", None, "net"),
        P(None, "net"),
        P(None, "net"),
        P("net"),
        P("net"),
        P("net"),
        P("ctg"),
        P("net"),
    )
    return jax.shard_map(
        body,
        mesh=mesh,
        in_specs=placed,
        out_specs=(P("ctg", None, "net"), P(None, "net")),
        check_vma=False,
    )
```

```python
import jax
import jax.numpy as jnp
from jax import lax
from jax.experimental import pallas as pl
from jax.experimental.pallas import tpu as pltpu
from jax.sharding import PartitionSpec as P

BUS_DEV = 4096
BR_DEV = 5632
G_DEV = 1280
RIM = 128
PERIODS = 16
TILES = BUS_DEV // RIM
BR_ROWS = BR_DEV // RIM
PART_ROWS = 48
SENT_ROWS = 208
PAIRS = TILES // 2
CASES = 4
ROWS = CASES * PERIODS
VMEM_LIMIT = 20 * 1024 * 1024
WIDE = 2 * RIM
SLOTS = 256
GROUPS = 64
WORK = 256
BF16 = jnp.bfloat16
F32 = jnp.float32


def split(value):
    high = value.astype(BF16)
    low = (value - high.astype(F32)).astype(BF16)
    return high, low


def dot_last(left, right):
    return lax.dot_general(
        left, right, (((1,), (1,)), ((), ())), preferred_element_type=F32
    )


def dot_plain(left, right):
    return jnp.dot(left, right, preferred_element_type=F32)


def whole(ref_space=pltpu.VMEM):
    return pl.BlockSpec(memory_space=ref_space)


def one_hot(rows, index):
    spots = lax.broadcasted_iota(jnp.int32, (rows, index.shape[1]), 0)
    return spots.astype(F32).astype(BF16) == index.astype(F32).astype(BF16)


def one_hot_turned(index, columns):
    spots = lax.broadcasted_iota(jnp.int32, (index.shape[0], columns), 1)
    return spots.astype(F32).astype(BF16) == index.astype(BF16)


def held_at(mask, values):
    return jnp.where(mask, values, jnp.zeros((), BF16))


def ones_at(mask):
    return held_at(mask, jnp.ones((), BF16))


def as_row(ref):
    return ref[...].reshape(1, ref.shape[0])


def pack_kernel(
    from_hbm, to_hbm, susc_hbm, field_hbm, out_ref, first_ref, from_ref, to_ref, susc_ref, sems
):
    moves = (
        (from_hbm, from_ref),
        (to_hbm, to_ref),
        (susc_hbm, susc_ref),
        (field_hbm.at[:, pl.ds(BUS_DEV - RIM, RIM)], out_ref.at[pl.ds(3 * PART_ROWS, ROWS), :]),
        (field_hbm.at[:, pl.ds(0, RIM)], first_ref),
    )
    copies = [pltpu.make_async_copy(*move, sems.at[k]) for k, move in enumerate(moves)]
    for copy in copies:
        copy.start()
    for part, ref in enumerate((from_ref, to_ref, susc_ref)):
        copies[part].wait()
        row = as_row(ref).astype(F32)
        for k in range(BR_ROWS):
            at = part * PART_ROWS + k
            out_ref[at : at + 1, :] = row[:, k * RIM : (k + 1) * RIM]
        out_ref[part * PART_ROWS + BR_ROWS : (part + 1) * PART_ROWS, :] = jnp.zeros(
            (PART_ROWS - BR_ROWS, RIM), F32
        )
    copies[3].wait()
    copies[4].wait()


def pack(from_bus, to_bus, susceptance, field):
    return pl.pallas_call(
        pack_kernel,
        in_specs=[whole(pltpu.HBM)] * 4,
        out_specs=[whole()] * 5,
        out_shape=[
            pltpu.VMEM((SENT_ROWS, RIM), F32),
            pltpu.VMEM((ROWS, RIM), F32),
            pltpu.VMEM((BR_DEV,), jnp.int32),
            pltpu.VMEM((BR_DEV,), jnp.int32),
            pltpu.VMEM((BR_DEV,), F32),
        ],
        scratch_shapes=[pltpu.SemaphoreType.DMA((5,))],
        compiler_params=pltpu.CompilerParams(vmem_limit_bytes=63 << 20),
        name="pack",
    )(from_bus, to_bus, susceptance, field)


def turned_tile(starts_row, to_row, high_row, low_row):
    starts = ones_at(one_hot(RIM, starts_row))
    hit = one_hot(RIM, to_row)
    high_row, low_row = high_row.astype(BF16), low_row.astype(BF16)
    ends = jnp.concatenate([held_at(hit, high_row), held_at(hit, low_row)], axis=0)
    both = dot_last(ends, starts)
    return both[:RIM] + both[RIM:]


def band_kernel(
    from_ref, to_ref, susc_ref, high_ref, low_ref, degree_ref, tiles, table
):
    base = lax.axis_index("net") * BUS_DEV
    from_local = as_row(from_ref) - base
    tile = from_local // RIM
    packed = ones_at(one_hot(TILES, tile))
    member = packed.astype(F32)
    chunks = BR_DEV // WORK
    rows = lax.broadcasted_iota(jnp.int32, (WORK, WORK), 0)
    cols = lax.broadcasted_iota(jnp.int32, (WORK, WORK), 1)
    upto = jnp.where(rows <= cols, 1.0, 0.0).astype(BF16)
    counts = dot_plain(
        jnp.concatenate([packed[:, c * WORK : (c + 1) * WORK] for c in range(chunks)], axis=0),
        upto,
    )
    seen = jnp.zeros((TILES, 1), F32)
    ranks = []
    for c in range(chunks):
        local = counts[c * TILES : (c + 1) * TILES]
        part = member[:, c * WORK : (c + 1) * WORK] * (local + seen)
        ranks.append(jnp.sum(part, axis=0, keepdims=True) - 1.0)
        seen = seen + local[:, WORK - 1 : WORK]
    rank = jnp.concatenate(ranks, axis=1).astype(jnp.int32)

    extra = jnp.maximum((seen.astype(jnp.int32) + (SLOTS - 1)) // SLOTS - 1, 0).astype(F32)
    sub = lax.broadcasted_iota(jnp.int32, (TILES, RIM), 0)
    lane = lax.broadcasted_iota(jnp.int32, (TILES, RIM), 1)
    extra_row = jnp.sum(jnp.where(sub == lane, extra, 0.0), axis=0, keepdims=True)
    extra_from = jnp.sum(jnp.where(lane < sub, extra_row, 0.0), axis=1, keepdims=True)
    extra_upto = extra_from + extra
    spill = jnp.sum(extra).astype(jnp.int32)
    spill_at = jnp.sum(member * extra_from, axis=0, keepdims=True).astype(jnp.int32)
    group = jnp.where(rank < SLOTS, tile, TILES + spill_at + rank // SLOTS - 1)
    group_hit = one_hot(GROUPS, group)
    slot_hit = ones_at(one_hot(SLOTS, rank % SLOTS))
    features = (
        (from_local % RIM).astype(F32).astype(BF16),
        ((as_row(to_ref) - base) % RIM).astype(F32).astype(BF16),
        *split(as_row(susc_ref)),
    )
    table[...] = dot_last(
        jnp.concatenate([held_at(group_hit, value) for value in features], axis=0), slot_hit
    )

    def group_tile(at):
        rows = [table[pl.ds(part * GROUPS + at, 1), :] for part in range(4)]
        return turned_tile(*rows)

    @pl.when(spill > 0)
    def _():
        tiles[...] = jnp.zeros_like(tiles)

        @pl.loop(0, spill)
        def _(step):
            passed = jnp.where(extra_upto <= step.astype(F32), 1.0, 0.0)
            owner = jnp.sum(passed).astype(jnp.int32)
            tiles[owner] = tiles[owner] + group_tile(TILES + step)

    rows = lax.broadcasted_iota(jnp.int32, (RIM, RIM), 0)
    cols = lax.broadcasted_iota(jnp.int32, (RIM, RIM), 1)
    later = cols > rows
    narrow = [x.astype(F32).astype(BF16) for x in (rows, cols)]
    above, below = narrow[1] > narrow[0], narrow[1] < narrow[0]
    zero = jnp.zeros((RIM, RIM), BF16)
    carried = jnp.zeros((1, RIM), F32)
    for at in range(TILES):
        pair, odd = at // 2, at % 2
        turned = group_tile(at) + jnp.where(spill > 0, tiles[at], 0.0)
        block = turned.T
        own = slice((1 + odd) * RIM, (2 + odd) * RIM)
        mine = slice(odd * RIM, (odd + 1) * RIM)
        other = slice((1 - odd) * RIM, (2 - odd) * RIM)
        for ref, part, back in zip((high_ref, low_ref), split(block), split(turned)):
            inside_part = jnp.where(above, part, jnp.where(below, back, zero))
            ahead_part = jnp.where(above, zero, part)
            back_part = jnp.where(below, zero, back)
            ref[pair, own, mine] = inside_part
            if odd == 0:
                ref[pair, 2 * RIM : 3 * RIM, mine] = back_part
                ref[pair, 3 * RIM :, mine] = zero
                ref[pair, RIM : 2 * RIM, other] = ahead_part
                if pair == 0:
                    ref[pair, :RIM, mine] = zero
            else:
                ref[pair, 3 * RIM :, mine] = back_part
                ref[pair, :RIM, mine] = zero
                if pair + 1 < PAIRS:
                    ref[pair + 1, :RIM, :RIM] = ahead_part
        inside = jnp.sum(jnp.where(later, block, 0.0), axis=0, keepdims=True)
        degree_ref[:, at * RIM : (at + 1) * RIM] = (
            inside + jnp.sum(turned, axis=0, keepdims=True) + carried
        )
        carried = jnp.sum(jnp.where(later, 0.0, block), axis=0, keepdims=True)


def build_band(from_bus, to_bus, susceptance):
    shape = pltpu.VMEM((PAIRS, 4 * RIM, 2 * RIM), BF16)
    return pl.pallas_call(
        band_kernel,
        in_specs=[whole()] * 3,
        out_specs=[whole()] * 3,
        out_shape=[shape, shape, pltpu.VMEM((1, BUS_DEV), F32)],
        scratch_shapes=[
            pltpu.VMEM((TILES, RIM, RIM), F32),
            pltpu.VMEM((4 * GROUPS, SLOTS), F32),
        ],
        compiler_params=pltpu.CompilerParams(vmem_limit_bytes=VMEM_LIMIT),
        cost_estimate=pl.CostEstimate(flops=8 << 30, bytes_accessed=16 << 20, transcendentals=0),
        name="band",
    )(from_bus, to_bus, susceptance)


def outage_row(from_at, to_at, start, width):
    spots = lax.broadcasted_iota(jnp.int32, (1, width), 1) + start
    return jnp.where(spots == from_at, 1.0, 0.0) - jnp.where(spots == to_at, 1.0, 0.0)


def apply_pairs(halo, inner, stacks, high_ref, low_ref, cross, degrees, ends, susc, emit):
    flows = [jnp.zeros((PERIODS, RIM), F32) for _ in range(CASES)]
    for tile in range(-1, TILES + 1):
        value = halo(tile) if tile in (-1, TILES) else inner(tile * RIM, RIM)
        high, low = split(value)
        cols = slice((tile + 1) * RIM, (tile + 2) * RIM)
        stacks[:ROWS, cols] = high
        stacks[ROWS:, cols] = low
        for case in range(CASES):
            mask = outage_row(*ends[case], (tile + 1) * RIM, RIM)
            flows[case] += value[case * PERIODS : (case + 1) * PERIODS] * mask
    drops = [
        susc[case] * jnp.sum(flows[case], axis=1, keepdims=True) for case in range(CASES)
    ]
    width = 2 * RIM
    for pair in range(PAIRS):
        near = stacks[:, pair * width : pair * width + 2 * width]
        sums = dot_plain(near, high_ref[pair]) + dot_plain(near, low_ref[pair])
        sums = sums[:ROWS] + sums[ROWS:]
        if pair == 0:
            outer = dot_plain(stacks[:, :RIM], cross)
            outer = outer[:ROWS] + outer[ROWS:]
            outer = outer[:, :RIM] + outer[:, RIM:]
            sums = sums + jnp.concatenate([outer, jnp.zeros((ROWS, RIM), F32)], axis=1)
        cols = slice(pair * width, (pair + 1) * width)
        result = degrees(cols) * inner(pair * width, width) - sums
        parts = []
        for case in range(CASES):
            mask = outage_row(*ends[case], pair * width + RIM, width)
            parts.append(result[case * PERIODS : (case + 1) * PERIODS] - drops[case] * mask)
        emit(pair, cols, jnp.concatenate(parts, axis=0))


def resid_kernel(
    outage_ref,
    field_ref,
    barrier_ref,
    high_ref,
    low_ref,
    own_degree_ref,
    own_ref,
    left_ref,
    right_ref,
    dispatch_ref,
    gen_ref,
    weighted_ref,
    first_ref,
    last_ref,
    partial_ref,
    cross_ref,
    degree_ref,
    ends_ref,
    stacks,
    inject,
    total,
):
    block = lax.axis_index("net")
    base = block * BUS_DEV
    keep = jnp.where(block > 0, 1.0, 0.0)
    shift = (base - RIM).astype(F32)
    starts, stops, values = [
        left_ref[part * PART_ROWS : (part + 1) * PART_ROWS] for part in range(3)
    ]
    starts, stops, values = starts - shift, stops - shift, values * keep
    crossing = stops >= RIM
    from_row, to_row, high_row, low_row = [
        jnp.concatenate([part[k : k + 1] for k in range(BR_ROWS)], axis=1)
        for part in (
            starts,
            stops - RIM,
            *[part.astype(F32) for part in split(jnp.where(crossing, values, 0.0))],
        )
    ]
    hit = one_hot(RIM, to_row)
    left_ends = jnp.concatenate(
        [held_at(hit, high_row.astype(BF16)), held_at(hit, low_row.astype(BF16))], axis=0
    )
    columns = starts.T
    turned_starts = jnp.concatenate(
        [ones_at(one_hot_turned(columns[:, k : k + 1], RIM)) for k in range(BR_ROWS)],
        axis=0,
    )
    both = dot_plain(left_ends, turned_starts)
    across = (both[:RIM] + both[RIM:]).T
    cross = jnp.concatenate(split(across), axis=1)
    cross_ref[...] = cross
    degree_ref[...] = own_degree_ref[...]
    degree_ref[:, :RIM] = own_degree_ref[:, :RIM] + jnp.sum(across, axis=0, keepdims=True)

    own_starts, own_stops, own_values = [
        own_ref[part * PART_ROWS : (part + 1) * PART_ROWS] for part in range(3)
    ]
    pairs = (
        (own_starts - shift, starts * keep),
        (own_stops - shift, stops * keep),
        (own_values, values),
    )
    branch = (
        lax.broadcasted_iota(jnp.int32, (PART_ROWS, RIM), 0) * RIM
        + lax.broadcasted_iota(jnp.int32, (PART_ROWS, RIM), 1)
        + block * BR_DEV
    )
    inside = lax.broadcasted_iota(jnp.int32, (PART_ROWS, RIM), 0) < BR_ROWS
    branch = jnp.where(inside, branch, -BR_DEV - 1)
    out_row = outage_ref[...].reshape(1, CASES)
    ends, susc = [], []
    for case in range(CASES):
        out = out_row[:, case : case + 1]
        own_hit = branch == out
        left_hit = branch == out + BR_DEV
        start, end, value = [
            jnp.sum(
                jnp.sum(
                    jnp.where(own_hit, own, 0.0) + jnp.where(left_hit, left, 0.0),
                    axis=0,
                    keepdims=True,
                ),
                axis=1,
                keepdims=True,
            )
            for own, left in pairs
        ]
        ends.append((start.astype(jnp.int32), end.astype(jnp.int32)))
        susc.append(value)
        for k, held in enumerate((start, end, value)):
            at = 4 * k + case
            ends_ref[at : at + 1, :] = jnp.broadcast_to(held, (1, RIM))

    gen = as_row(gen_ref) - base
    gen_pair = gen // WIDE
    gen_hits = [gen_pair.astype(F32).astype(BF16) == pair for pair in range(PAIRS)]
    gen_spots = ones_at(one_hot(WIDE, gen % WIDE))
    picked = jnp.concatenate(
        [held_at(hit, value) for value in split(dispatch_ref[...]) for hit in gen_hits], axis=0
    )
    spread = dot_last(picked, gen_spots)
    inject[...] = spread[: PAIRS * PERIODS] + spread[PAIRS * PERIODS :]

    def halo(tile):
        return left_ref[3 * PART_ROWS :] if tile < 0 else right_ref[...]

    def inner(start, width):
        return field_ref[:, start : start + width]

    def emit(pair, cols, result):
        rows = slice(pair * PERIODS, (pair + 1) * PERIODS)
        taken = inject[rows]
        resid = result - jnp.concatenate([taken] * CASES, axis=0)
        weighted = barrier_ref[:, cols].astype(F32) * resid
        weighted_ref[:, cols] = weighted
        if pair == 0:
            first_ref[...] = weighted[:, :RIM]
        if pair == PAIRS - 1:
            last_ref[...] = weighted[:, RIM:]
        total[rows] = (
            weighted[0:16] + weighted[16:32] + (weighted[32:48] + weighted[48:64])
        )

    def degrees(cols):
        return degree_ref[:, cols]

    apply_pairs(halo, inner, stacks, high_ref, low_ref, cross, degrees, ends, susc, emit)

    at_gens = jnp.zeros((PERIODS, G_DEV), F32)
    size = PAIRS * PERIODS // 2
    for part in range(2):
        high, low = split(total[part * size : (part + 1) * size])
        both = dot_plain(jnp.concatenate([high, low], axis=0), gen_spots)
        for k in range(PAIRS // 2):
            rows = slice(k * PERIODS, (k + 1) * PERIODS)
            value = both[rows] + both[size + k * PERIODS : size + (k + 1) * PERIODS]
            at_gens += jnp.where(gen_pair == part * (PAIRS // 2) + k, value, 0.0)
    partial_ref[...] = at_gens


def residuals(outage, field, barrier, band, own, halos, dispatch, gen_bus):
    tile = pltpu.VMEM((ROWS, RIM), F32)
    return pl.pallas_call(
        resid_kernel,
        in_specs=[whole()] * 11,
        out_specs=[whole()] * 7,
        out_shape=[
            pltpu.VMEM((ROWS, BUS_DEV), F32),
            tile,
            tile,
            pltpu.VMEM((PERIODS, G_DEV), F32),
            pltpu.VMEM((RIM, 2 * RIM), BF16),
            pltpu.VMEM((1, BUS_DEV), F32),
            pltpu.VMEM((16, RIM), F32),
        ],
        scratch_shapes=[
            pltpu.VMEM((2 * ROWS, BUS_DEV + 2 * RIM), BF16),
            pltpu.VMEM((PAIRS * PERIODS, WIDE), F32),
            pltpu.VMEM((PAIRS * PERIODS, WIDE), F32),
        ],
        compiler_params=pltpu.CompilerParams(vmem_limit_bytes=VMEM_LIMIT),
        cost_estimate=pl.CostEstimate(flops=4 << 30, bytes_accessed=8 << 20, transcendentals=0),
        name="resid",
    )(outage, field, barrier, *band, own, *halos, dispatch, gen_bus)


def angle_kernel(
    weighted_ref,
    field_ref,
    reg_ref,
    high_ref,
    low_ref,
    cross_ref,
    degree_ref,
    ends_ref,
    left_ref,
    right_ref,
    out_ref,
    stacks,
):
    ends, susc = [], []
    for case in range(CASES):
        held = [ends_ref[4 * k + case : 4 * k + case + 1, 0:1] for k in range(3)]
        ends.append((held[0].astype(jnp.int32), held[1].astype(jnp.int32)))
        susc.append(held[2])

    def halo(tile):
        return left_ref[...] if tile < 0 else right_ref[...]

    def inner(start, width):
        return weighted_ref[:, start : start + width]

    def emit(pair, cols, result):
        scale = jnp.concatenate([reg_ref[:, cols]] * CASES, axis=0)
        out_ref[:, cols] = result + scale * field_ref[:, cols]

    def degrees(cols):
        return degree_ref[:, cols]

    apply_pairs(
        halo, inner, stacks, high_ref, low_ref, cross_ref[...], degrees, ends, susc, emit
    )


def angles(weighted, field, reg, band, cross, degree, ends, halos):
    return pl.pallas_call(
        angle_kernel,
        in_specs=[whole()] * 10,
        out_specs=whole(),
        out_shape=jax.ShapeDtypeStruct((ROWS, BUS_DEV), F32),
        scratch_shapes=[pltpu.VMEM((2 * ROWS, BUS_DEV + 2 * RIM), BF16)],
        compiler_params=pltpu.CompilerParams(vmem_limit_bytes=VMEM_LIMIT),
        cost_estimate=pl.CostEstimate(flops=4 << 30, bytes_accessed=8 << 20, transcendentals=0),
        name="angles",
    )(weighted, field, reg, *band, cross, degree, ends, *halos)


def shifted(block, distance):
    size = lax.axis_size("net")
    return lax.ppermute(block, "net", [(i, (i + distance) % size) for i in range(size)])


def sum_cases(value, masks_of_steps):
    size = lax.axis_size("ctg")
    for masks in masks_of_steps:
        parts = [
            lax.ppermute(value, "ctg", [(i, i ^ mask) for i in range(size)]) for mask in masks
        ]
        for part in parts:
            value = value + part
    return value


def body(
    angle_dir,
    dispatch_dir,
    barrier,
    angle_reg,
    dispatch_reg,
    susceptance,
    from_bus,
    to_bus,
    outage,
    gen_bus,
):
    field = angle_dir.reshape(ROWS, BUS_DEV)
    weights = barrier.reshape(ROWS, BUS_DEV)
    packed, lead, *raw = pack(from_bus, to_bus, susceptance, field)
    left = shifted(packed, 1)
    right = shifted(lead, -1)
    high, low, own_degree = build_band(*raw)
    weighted, first, last, partial, cross, degree, ends = residuals(
        outage,
        field,
        weights,
        (high, low, own_degree),
        packed,
        (left, right),
        dispatch_dir,
        gen_bus,
    )
    partial = sum_cases(partial, ((8,), (16,)))
    partial, *halos = lax.optimization_barrier(
        (partial, shifted(last, 1), shifted(first, -1))
    )
    summed = sum_cases(partial, ((1, 2, 3), (4,), (40,)))
    angle_out = angles(
        weighted, field, angle_reg, (high, low), cross, degree, ends, halos
    )
    case_count = float(CASES * lax.axis_size("ctg"))
    dispatch_out = dispatch_reg * dispatch_dir - summed / case_count
    return (angle_out.reshape(angle_dir.shape), dispatch_out)


def solution(mesh):
    placed = (
        P("ctg", None, "net"),
        P(None, "net"),
        P("ctg", None, "net"),
        P(None, "net"),
        P(None, "net"),
        P("net"),
        P("net"),
        P("net"),
        P("ctg"),
        P("net"),
    )
    return jax.shard_map(
        body,
        mesh=mesh,
        in_specs=placed,
        out_specs=(P("ctg", None, "net"), P(None, "net")),
        check_vma=False,
    )
```

```python
import jax
import jax.numpy as jnp
from jax import lax
from jax.experimental import pallas as pl
from jax.experimental.pallas import tpu as pltpu
from jax.sharding import PartitionSpec as P

BUS_DEV = 4096
BR_DEV = 5632
G_DEV = 1280
RIM = 128
PERIODS = 16
TILES = BUS_DEV // RIM
BR_ROWS = BR_DEV // RIM
PART_ROWS = 48
SENT_ROWS = 208
PAIRS = TILES // 2
CASES = 4
ROWS = CASES * PERIODS
VMEM_LIMIT = 20 * 1024 * 1024
WIDE = 2 * RIM
SLOTS = 256
GROUPS = 64
WORK = 256
BF16 = jnp.bfloat16
F32 = jnp.float32


def split(value):
    high = value.astype(BF16)
    low = (value - high.astype(F32)).astype(BF16)
    return high, low


def dot_last(left, right):
    return lax.dot_general(
        left, right, (((1,), (1,)), ((), ())), preferred_element_type=F32
    )


def dot_plain(left, right):
    return jnp.dot(left, right, preferred_element_type=F32)


def whole(ref_space=pltpu.VMEM):
    return pl.BlockSpec(memory_space=ref_space)


def one_hot(rows, index):
    spots = lax.broadcasted_iota(jnp.int32, (rows, index.shape[1]), 0)
    return spots.astype(F32).astype(BF16) == index.astype(F32).astype(BF16)


def one_hot_turned(index, columns):
    spots = lax.broadcasted_iota(jnp.int32, (index.shape[0], columns), 1)
    return spots.astype(F32).astype(BF16) == index.astype(BF16)


def held_at(mask, values):
    return jnp.where(mask, values, jnp.zeros((), BF16))


def ones_at(mask):
    return held_at(mask, jnp.ones((), BF16))


def as_row(ref):
    return ref[...].reshape(1, ref.shape[0])


def pack_kernel(
    from_hbm, to_hbm, susc_hbm, field_hbm, out_ref, first_ref, from_ref, to_ref, susc_ref, sems
):
    moves = (
        (from_hbm, from_ref),
        (to_hbm, to_ref),
        (susc_hbm, susc_ref),
        (field_hbm.at[:, pl.ds(BUS_DEV - RIM, RIM)], out_ref.at[pl.ds(3 * PART_ROWS, ROWS), :]),
        (field_hbm.at[:, pl.ds(0, RIM)], first_ref),
    )
    copies = [pltpu.make_async_copy(*move, sems.at[k]) for k, move in enumerate(moves)]
    for copy in copies:
        copy.start()
    for part, ref in enumerate((from_ref, to_ref, susc_ref)):
        copies[part].wait()
        row = as_row(ref).astype(F32)
        for k in range(BR_ROWS):
            at = part * PART_ROWS + k
            out_ref[at : at + 1, :] = row[:, k * RIM : (k + 1) * RIM]
        out_ref[part * PART_ROWS + BR_ROWS : (part + 1) * PART_ROWS, :] = jnp.zeros(
            (PART_ROWS - BR_ROWS, RIM), F32
        )
    copies[3].wait()
    copies[4].wait()


def pack(from_bus, to_bus, susceptance, field):
    return pl.pallas_call(
        pack_kernel,
        in_specs=[whole(pltpu.HBM)] * 4,
        out_specs=[whole()] * 5,
        out_shape=[
            pltpu.VMEM((SENT_ROWS, RIM), F32),
            pltpu.VMEM((ROWS, RIM), F32),
            pltpu.VMEM((BR_DEV,), jnp.int32),
            pltpu.VMEM((BR_DEV,), jnp.int32),
            pltpu.VMEM((BR_DEV,), F32),
        ],
        scratch_shapes=[pltpu.SemaphoreType.DMA((5,))],
        compiler_params=pltpu.CompilerParams(vmem_limit_bytes=63 << 20),
        name="pack",
    )(from_bus, to_bus, susceptance, field)


def turned_tile(starts_row, to_row, high_row, low_row):
    starts = ones_at(one_hot(RIM, starts_row))
    hit = one_hot(RIM, to_row)
    high_row, low_row = high_row.astype(BF16), low_row.astype(BF16)
    ends = jnp.concatenate([held_at(hit, high_row), held_at(hit, low_row)], axis=0)
    both = dot_last(ends, starts)
    return both[:RIM] + both[RIM:]


def band_kernel(
    from_ref, to_ref, susc_ref, high_ref, low_ref, degree_ref, tiles, table
):
    base = lax.axis_index("net") * BUS_DEV
    from_local = as_row(from_ref) - base
    tile = from_local // RIM
    packed = ones_at(one_hot(TILES, tile))
    member = packed.astype(F32)
    chunks = BR_DEV // WORK
    rows = lax.broadcasted_iota(jnp.int32, (WORK, WORK), 0)
    cols = lax.broadcasted_iota(jnp.int32, (WORK, WORK), 1)
    upto = jnp.where(rows <= cols, 1.0, 0.0).astype(BF16)
    counts = dot_plain(
        jnp.concatenate([packed[:, c * WORK : (c + 1) * WORK] for c in range(chunks)], axis=0),
        upto,
    )
    seen = jnp.zeros((TILES, 1), F32)
    ranks = []
    for c in range(chunks):
        local = counts[c * TILES : (c + 1) * TILES]
        part = member[:, c * WORK : (c + 1) * WORK] * (local + seen)
        ranks.append(jnp.sum(part, axis=0, keepdims=True) - 1.0)
        seen = seen + local[:, WORK - 1 : WORK]
    rank = jnp.concatenate(ranks, axis=1).astype(jnp.int32)

    extra = jnp.maximum((seen.astype(jnp.int32) + (SLOTS - 1)) // SLOTS - 1, 0).astype(F32)
    sub = lax.broadcasted_iota(jnp.int32, (TILES, RIM), 0)
    lane = lax.broadcasted_iota(jnp.int32, (TILES, RIM), 1)
    extra_row = jnp.sum(jnp.where(sub == lane, extra, 0.0), axis=0, keepdims=True)
    extra_from = jnp.sum(jnp.where(lane < sub, extra_row, 0.0), axis=1, keepdims=True)
    extra_upto = extra_from + extra
    spill = jnp.sum(extra).astype(jnp.int32)
    spill_at = jnp.sum(member * extra_from, axis=0, keepdims=True).astype(jnp.int32)
    group = jnp.where(rank < SLOTS, tile, TILES + spill_at + rank // SLOTS - 1)
    group_hit = one_hot(GROUPS, group)
    slot_hit = ones_at(one_hot(SLOTS, rank % SLOTS))
    features = (
        (from_local % RIM).astype(F32).astype(BF16),
        ((as_row(to_ref) - base) % RIM).astype(F32).astype(BF16),
        *split(as_row(susc_ref)),
    )
    table[...] = dot_last(
        jnp.concatenate([held_at(group_hit, value) for value in features], axis=0), slot_hit
    )

    def group_tile(at):
        rows = [table[pl.ds(part * GROUPS + at, 1), :] for part in range(4)]
        return turned_tile(*rows)

    @pl.when(spill > 0)
    def _():
        tiles[...] = jnp.zeros_like(tiles)

        @pl.loop(0, spill)
        def _(step):
            passed = jnp.where(extra_upto <= step.astype(F32), 1.0, 0.0)
            owner = jnp.sum(passed).astype(jnp.int32)
            tiles[owner] = tiles[owner] + group_tile(TILES + step)

    rows = lax.broadcasted_iota(jnp.int32, (RIM, RIM), 0)
    cols = lax.broadcasted_iota(jnp.int32, (RIM, RIM), 1)
    later = cols > rows
    narrow = [x.astype(F32).astype(BF16) for x in (rows, cols)]
    above, below = narrow[1] > narrow[0], narrow[1] < narrow[0]
    zero = jnp.zeros((RIM, RIM), BF16)
    def finish(spilled):
        carried = jnp.zeros((1, RIM), F32)
        for at in range(TILES):
            pair, odd = at // 2, at % 2
            turned = group_tile(at)
            if spilled:
                turned = turned + tiles[at]
            block = turned.T
            own = slice((1 + odd) * RIM, (2 + odd) * RIM)
            mine = slice(odd * RIM, (odd + 1) * RIM)
            other = slice((1 - odd) * RIM, (2 - odd) * RIM)
            for ref, part, back in zip((high_ref, low_ref), split(block), split(turned)):
                inside_part = jnp.where(above, part, jnp.where(below, back, zero))
                ahead_part = jnp.where(above, zero, part)
                back_part = jnp.where(below, zero, back)
                ref[pair, own, mine] = inside_part
                if odd == 0:
                    ref[pair, 2 * RIM : 3 * RIM, mine] = back_part
                    ref[pair, 3 * RIM :, mine] = zero
                    ref[pair, RIM : 2 * RIM, other] = ahead_part
                    if pair == 0:
                        ref[pair, :RIM, mine] = zero
                else:
                    ref[pair, 3 * RIM :, mine] = back_part
                    ref[pair, :RIM, mine] = zero
                    if pair + 1 < PAIRS:
                        ref[pair + 1, :RIM, :RIM] = ahead_part
            inside = jnp.sum(jnp.where(later, block, 0.0), axis=0, keepdims=True)
            degree_ref[:, at * RIM : (at + 1) * RIM] = (
                inside + jnp.sum(turned, axis=0, keepdims=True) + carried
            )
            carried = jnp.sum(jnp.where(later, 0.0, block), axis=0, keepdims=True)

    pl.when(spill == 0)(lambda: finish(False))
    pl.when(spill > 0)(lambda: finish(True))


def build_band(from_bus, to_bus, susceptance):
    shape = pltpu.VMEM((PAIRS, 4 * RIM, 2 * RIM), BF16)
    return pl.pallas_call(
        band_kernel,
        in_specs=[whole()] * 3,
        out_specs=[whole()] * 3,
        out_shape=[shape, shape, pltpu.VMEM((1, BUS_DEV), F32)],
        scratch_shapes=[
            pltpu.VMEM((TILES, RIM, RIM), F32),
            pltpu.VMEM((4 * GROUPS, SLOTS), F32),
        ],
        compiler_params=pltpu.CompilerParams(vmem_limit_bytes=VMEM_LIMIT),
        cost_estimate=pl.CostEstimate(flops=8 << 30, bytes_accessed=16 << 20, transcendentals=0),
        name="band",
    )(from_bus, to_bus, susceptance)


def outage_row(from_at, to_at, start, width):
    spots = lax.broadcasted_iota(jnp.int32, (1, width), 1) + start
    return jnp.where(spots == from_at, 1.0, 0.0) - jnp.where(spots == to_at, 1.0, 0.0)


def apply_pairs(halo, inner, stacks, high_ref, low_ref, cross, degrees, ends, susc, emit):
    flows = [jnp.zeros((PERIODS, RIM), F32) for _ in range(CASES)]
    for tile in range(-1, TILES + 1):
        value = halo(tile) if tile in (-1, TILES) else inner(tile * RIM, RIM)
        high, low = split(value)
        cols = slice((tile + 1) * RIM, (tile + 2) * RIM)
        stacks[:ROWS, cols] = high
        stacks[ROWS:, cols] = low
        for case in range(CASES):
            mask = outage_row(*ends[case], (tile + 1) * RIM, RIM)
            flows[case] += value[case * PERIODS : (case + 1) * PERIODS] * mask
    drops = [
        susc[case] * jnp.sum(flows[case], axis=1, keepdims=True) for case in range(CASES)
    ]
    width = 2 * RIM
    for pair in range(PAIRS):
        near = stacks[:, pair * width : pair * width + 2 * width]
        sums = dot_plain(near, high_ref[pair]) + dot_plain(near, low_ref[pair])
        sums = sums[:ROWS] + sums[ROWS:]
        if pair == 0:
            outer = dot_plain(stacks[:, :RIM], cross)
            outer = outer[:ROWS] + outer[ROWS:]
            outer = outer[:, :RIM] + outer[:, RIM:]
            sums = sums + jnp.concatenate([outer, jnp.zeros((ROWS, RIM), F32)], axis=1)
        cols = slice(pair * width, (pair + 1) * width)
        result = degrees(cols) * inner(pair * width, width) - sums
        parts = []
        for case in range(CASES):
            mask = outage_row(*ends[case], pair * width + RIM, width)
            parts.append(result[case * PERIODS : (case + 1) * PERIODS] - drops[case] * mask)
        emit(pair, cols, jnp.concatenate(parts, axis=0))


def resid_kernel(
    outage_ref,
    field_ref,
    barrier_ref,
    high_ref,
    low_ref,
    own_degree_ref,
    own_ref,
    left_ref,
    right_ref,
    dispatch_ref,
    gen_ref,
    weighted_ref,
    first_ref,
    last_ref,
    partial_ref,
    cross_ref,
    degree_ref,
    ends_ref,
    stacks,
    inject,
    total,
):
    block = lax.axis_index("net")
    base = block * BUS_DEV
    keep = jnp.where(block > 0, 1.0, 0.0)
    shift = (base - RIM).astype(F32)
    starts, stops, values = [
        left_ref[part * PART_ROWS : (part + 1) * PART_ROWS] for part in range(3)
    ]
    starts, stops, values = starts - shift, stops - shift, values * keep
    crossing = stops >= RIM
    from_row, to_row, high_row, low_row = [
        jnp.concatenate([part[k : k + 1] for k in range(BR_ROWS)], axis=1)
        for part in (
            starts,
            stops - RIM,
            *[part.astype(F32) for part in split(jnp.where(crossing, values, 0.0))],
        )
    ]
    hit = one_hot(RIM, to_row)
    left_ends = jnp.concatenate(
        [held_at(hit, high_row.astype(BF16)), held_at(hit, low_row.astype(BF16))], axis=0
    )
    columns = starts.T
    turned_starts = jnp.concatenate(
        [ones_at(one_hot_turned(columns[:, k : k + 1], RIM)) for k in range(BR_ROWS)],
        axis=0,
    )
    both = dot_plain(left_ends, turned_starts)
    across = (both[:RIM] + both[RIM:]).T
    cross = jnp.concatenate(split(across), axis=1)
    cross_ref[...] = cross
    degree_ref[...] = own_degree_ref[...]
    degree_ref[:, :RIM] = own_degree_ref[:, :RIM] + jnp.sum(across, axis=0, keepdims=True)

    own_starts, own_stops, own_values = [
        own_ref[part * PART_ROWS : (part + 1) * PART_ROWS] for part in range(3)
    ]
    pairs = (
        (own_starts - shift, starts * keep),
        (own_stops - shift, stops * keep),
        (own_values, values),
    )
    branch = (
        lax.broadcasted_iota(jnp.int32, (PART_ROWS, RIM), 0) * RIM
        + lax.broadcasted_iota(jnp.int32, (PART_ROWS, RIM), 1)
        + block * BR_DEV
    )
    inside = lax.broadcasted_iota(jnp.int32, (PART_ROWS, RIM), 0) < BR_ROWS
    branch = jnp.where(inside, branch, -BR_DEV - 1)
    out_row = outage_ref[...].reshape(1, CASES)
    ends, susc = [], []
    for case in range(CASES):
        out = out_row[:, case : case + 1]
        own_hit = branch == out
        left_hit = branch == out + BR_DEV
        start, end, value = [
            jnp.sum(
                jnp.sum(
                    jnp.where(own_hit, own, 0.0) + jnp.where(left_hit, left, 0.0),
                    axis=0,
                    keepdims=True,
                ),
                axis=1,
                keepdims=True,
            )
            for own, left in pairs
        ]
        ends.append((start.astype(jnp.int32), end.astype(jnp.int32)))
        susc.append(value)
        for k, held in enumerate((start, end, value)):
            at = 4 * k + case
            ends_ref[at : at + 1, :] = jnp.broadcast_to(held, (1, RIM))

    gen = as_row(gen_ref) - base
    gen_pair = gen // WIDE
    gen_hits = [gen_pair.astype(F32).astype(BF16) == pair for pair in range(PAIRS)]
    gen_spots = ones_at(one_hot(WIDE, gen % WIDE))
    picked = jnp.concatenate(
        [held_at(hit, value) for value in split(dispatch_ref[...]) for hit in gen_hits], axis=0
    )
    spread = dot_last(picked, gen_spots)
    inject[...] = spread[: PAIRS * PERIODS] + spread[PAIRS * PERIODS :]

    def halo(tile):
        return left_ref[3 * PART_ROWS :] if tile < 0 else right_ref[...]

    def inner(start, width):
        return field_ref[:, start : start + width]

    def emit(pair, cols, result):
        rows = slice(pair * PERIODS, (pair + 1) * PERIODS)
        taken = inject[rows]
        resid = result - jnp.concatenate([taken] * CASES, axis=0)
        weighted = barrier_ref[:, cols].astype(F32) * resid
        weighted_ref[:, cols] = weighted
        if pair == 0:
            first_ref[...] = weighted[:, :RIM]
        if pair == PAIRS - 1:
            last_ref[...] = weighted[:, RIM:]
        total[rows] = (
            weighted[0:16] + weighted[16:32] + (weighted[32:48] + weighted[48:64])
        )

    def degrees(cols):
        return degree_ref[:, cols]

    apply_pairs(halo, inner, stacks, high_ref, low_ref, cross, degrees, ends, susc, emit)

    at_gens = jnp.zeros((PERIODS, G_DEV), F32)
    size = PAIRS * PERIODS // 2
    for part in range(2):
        high, low = split(total[part * size : (part + 1) * size])
        both = dot_plain(jnp.concatenate([high, low], axis=0), gen_spots)
        for k in range(PAIRS // 2):
            rows = slice(k * PERIODS, (k + 1) * PERIODS)
            value = both[rows] + both[size + k * PERIODS : size + (k + 1) * PERIODS]
            at_gens += jnp.where(gen_pair == part * (PAIRS // 2) + k, value, 0.0)
    partial_ref[...] = at_gens


def residuals(outage, field, barrier, band, own, halos, dispatch, gen_bus):
    tile = pltpu.VMEM((ROWS, RIM), F32)
    return pl.pallas_call(
        resid_kernel,
        in_specs=[whole()] * 11,
        out_specs=[whole()] * 7,
        out_shape=[
            pltpu.VMEM((ROWS, BUS_DEV), F32),
            tile,
            tile,
            pltpu.VMEM((PERIODS, G_DEV), F32),
            pltpu.VMEM((RIM, 2 * RIM), BF16),
            pltpu.VMEM((1, BUS_DEV), F32),
            pltpu.VMEM((16, RIM), F32),
        ],
        scratch_shapes=[
            pltpu.VMEM((2 * ROWS, BUS_DEV + 2 * RIM), BF16),
            pltpu.VMEM((PAIRS * PERIODS, WIDE), F32),
            pltpu.VMEM((PAIRS * PERIODS, WIDE), F32),
        ],
        compiler_params=pltpu.CompilerParams(vmem_limit_bytes=VMEM_LIMIT),
        cost_estimate=pl.CostEstimate(flops=4 << 30, bytes_accessed=8 << 20, transcendentals=0),
        name="resid",
    )(outage, field, barrier, *band, own, *halos, dispatch, gen_bus)


def angle_kernel(
    weighted_ref,
    field_ref,
    reg_ref,
    high_ref,
    low_ref,
    cross_ref,
    degree_ref,
    ends_ref,
    left_ref,
    right_ref,
    out_ref,
    stacks,
):
    ends, susc = [], []
    for case in range(CASES):
        held = [ends_ref[4 * k + case : 4 * k + case + 1, 0:1] for k in range(3)]
        ends.append((held[0].astype(jnp.int32), held[1].astype(jnp.int32)))
        susc.append(held[2])

    def halo(tile):
        return left_ref[...] if tile < 0 else right_ref[...]

    def inner(start, width):
        return weighted_ref[:, start : start + width]

    def emit(pair, cols, result):
        scale = jnp.concatenate([reg_ref[:, cols]] * CASES, axis=0)
        out_ref[:, cols] = result + scale * field_ref[:, cols]

    def degrees(cols):
        return degree_ref[:, cols]

    apply_pairs(
        halo, inner, stacks, high_ref, low_ref, cross_ref[...], degrees, ends, susc, emit
    )


def angles(weighted, field, reg, band, cross, degree, ends, halos):
    return pl.pallas_call(
        angle_kernel,
        in_specs=[whole()] * 10,
        out_specs=whole(),
        out_shape=jax.ShapeDtypeStruct((ROWS, BUS_DEV), F32),
        scratch_shapes=[pltpu.VMEM((2 * ROWS, BUS_DEV + 2 * RIM), BF16)],
        compiler_params=pltpu.CompilerParams(vmem_limit_bytes=VMEM_LIMIT),
        cost_estimate=pl.CostEstimate(flops=4 << 30, bytes_accessed=8 << 20, transcendentals=0),
        name="angles",
    )(weighted, field, reg, *band, cross, degree, ends, *halos)


def shifted(block, distance):
    size = lax.axis_size("net")
    return lax.ppermute(block, "net", [(i, (i + distance) % size) for i in range(size)])


def sum_cases(value, masks_of_steps):
    size = lax.axis_size("ctg")
    for masks in masks_of_steps:
        parts = [
            lax.ppermute(value, "ctg", [(i, i ^ mask) for i in range(size)]) for mask in masks
        ]
        for part in parts:
            value = value + part
    return value


def body(
    angle_dir,
    dispatch_dir,
    barrier,
    angle_reg,
    dispatch_reg,
    susceptance,
    from_bus,
    to_bus,
    outage,
    gen_bus,
):
    field = angle_dir.reshape(ROWS, BUS_DEV)
    weights = barrier.reshape(ROWS, BUS_DEV)
    packed, lead, *raw = pack(from_bus, to_bus, susceptance, field)
    left = shifted(packed, 1)
    right = shifted(lead, -1)
    high, low, own_degree = build_band(*raw)
    weighted, first, last, partial, cross, degree, ends = residuals(
        outage,
        field,
        weights,
        (high, low, own_degree),
        packed,
        (left, right),
        dispatch_dir,
        gen_bus,
    )
    partial = sum_cases(partial, ((8,), (16,)))
    partial, *halos = lax.optimization_barrier(
        (partial, shifted(last, 1), shifted(first, -1))
    )
    summed = sum_cases(partial, ((1, 2, 3), (4,), (40,)))
    angle_out = angles(
        weighted, field, angle_reg, (high, low), cross, degree, ends, halos
    )
    case_count = float(CASES * lax.axis_size("ctg"))
    dispatch_out = dispatch_reg * dispatch_dir - summed / case_count
    return (angle_out.reshape(angle_dir.shape), dispatch_out)


def solution(mesh):
    placed = (
        P("ctg", None, "net"),
        P(None, "net"),
        P("ctg", None, "net"),
        P(None, "net"),
        P(None, "net"),
        P("net"),
        P("net"),
        P("net"),
        P("ctg"),
        P("net"),
    )
    return jax.shard_map(
        body,
        mesh=mesh,
        in_specs=placed,
        out_specs=(P("ctg", None, "net"), P(None, "net")),
        check_vma=False,
    )
```
